256 devices in a mesh: lon: 32 (over z_lo, y, core), mem: 8 (over z_hi, x).
Axes of the slice: x: 4, y: 4, z: 8 (z_hi: 2, z_lo: 4; z = z_hi * 4 + z_lo), core: 2. Of those that a mesh axis runs over, the one named last changes fastest.
Arguments:
- anomalies: bfloat16 [64, 512, 8192], P('mem', None, 'lon'), may hold values from -6 to 6
- increment: bfloat16 [512, 8192], P(None, 'lon'), may hold values from -6 to 6
- spectral_taper: float32 [8192], replicated, may hold values from 0.05 to 1
Outputs:
- covariance_product: float32 [512, 8192], P(None, 'lon')
The draws below stay inside these ranges and needn't reach their ends.
All inputs are finite; a program needn't handle non-finite values.
Results may differ from the reference program's by a relative error of at most 0.0011.
Values may be sent and summed in bfloat16 or wider, within the bound.
A program may use at most 128 MiB of HBM per device.

```python
import math
import jax
import jax.numpy as jnp
from jax import lax

NLON = 8192
MEMBERS = 64
LAT = 512


def levels(rng, shape, shards, least, high):
    gain = 1.0
    for position, shards_of in shards:
        steps = jax.random.uniform(jax.random.fold_in(jax.random.fold_in(rng, 6), position), (shards_of,), jnp.float32, least / len(shards), high / len(shards))
        gain = gain * jnp.repeat(jnp.exp(steps), shape[position] // shards_of).reshape((-1,) + (1,) * (len(shape) - 1 - position))
    return gain


def centred(stream_key, extent, width, most, pieces=(), dtype=jnp.bfloat16):
    array = width * jax.random.normal(stream_key, extent, jnp.float32)
    if pieces:
        array = array * levels(stream_key, extent, pieces, -0.22, 0.18)
    return jnp.clip(array, -most, most).astype(dtype)


def setup_inputs(seed: int = 0) -> dict:
    seeds = jax.random.split(jax.random.key(seed), 4)
    return {
        "anomalies": centred(seeds[0], (MEMBERS, LAT, NLON), 1.0, 6.0, ((0, 8), (2, 32))),
        "increment": centred(seeds[1], (LAT, NLON), 1.0, 6.0, ((1, 32),)),
        "spectral_taper": jnp.clip(jnp.exp(jax.random.uniform(seeds[2], (NLON,), jnp.float32, math.log(0.05), math.log(1.0))), 0.05, 1.0),
    }


def reference(anomalies, increment, spectral_taper):
    field = increment.astype(jnp.float32)

    def accumulate(summed, member):
        values = member.astype(jnp.float32)
        products = (values * field).astype(jnp.bfloat16)
        products = lax.optimization_barrier(products).astype(jnp.float32)
        spectra = jnp.fft.fft(products, axis=-1) * spectral_taper
        localized = jnp.real(jnp.fft.ifft(spectra, axis=-1)).astype(jnp.bfloat16)
        return summed + values * localized.astype(jnp.float32), None

    start = jnp.zeros(increment.shape, jnp.float32)
    summed, unused = lax.scan(accumulate, start, anomalies)
    return summed / (MEMBERS - 1)
```

```python
import functools
import math

import jax
import jax.numpy as jnp
import numpy as np
from jax import lax
from jax.experimental import pallas as pl
from jax.experimental.pallas import tpu as pltpu
from jax.sharding import PartitionSpec as P

MESH = pl.DeviceIdType.MESH
NLON = 8192
BLOCKS = 64
WIDE = 128
HALF = BLOCKS // 2
LONS = 32
XS = 4
LATS = 16
CHUNKS = 2
PER = LATS // CHUNKS
MEMBERS = 8
ROWS = PER * MEMBERS
PAIRS = MEMBERS // 2
F32 = jnp.float32
BF16 = jnp.bfloat16


def tables():
    s = np.arange(WIDE)[:, None]
    r = np.arange(BLOCKS)[None, :]
    first = 2 * math.pi * (s * r % BLOCKS) / BLOCKS
    first = np.concatenate([np.cos(first), np.sin(first)], 0)
    c = np.arange(WIDE)[None, :]
    twist = 2 * math.pi * (s * c % NLON) / NLON
    twist = np.stack([np.cos(twist), np.sin(twist)])
    d = np.arange(BLOCKS)[:, None]
    back = 2 * math.pi * (d * c % BLOCKS) / BLOCKS
    back = np.stack([np.cos(back), np.sin(back)]) / (NLON * BLOCKS)
    f = np.arange(40)[:, None]
    d = np.arange(BLOCKS)[None, :]
    here = 2 * math.pi * (f * d % BLOCKS) / BLOCKS
    there = 2 * math.pi * (f * (d + 1) % BLOCKS) / BLOCKS
    again = np.stack([np.cos(here), -np.sin(here), np.cos(there), -np.sin(there)])
    return [np.asarray(t, np.float32) for t in (first, twist, back, again)]


def dft4(x):
    (ar, ai), (br, bi), (cr, ci), (dr, di) = x
    er, ei, fr, fi = ar + cr, ai + ci, ar - cr, ai - ci
    gr, gi, hr, hi = br + dr, bi + di, br - dr, bi - di
    return [(er + gr, ei + gi), (fr + hi, fi - hr), (er - gr, ei - gi), (fr - hi, fi + hr)]


def dft8(x):
    even, odd = dft4(x[0::2]), dft4(x[1::2])
    root = math.sqrt(0.5)
    (ar, ai), (br, bi), (cr, ci), (dr, di) = odd
    turned = [
        (ar, ai),
        ((br + bi) * root, (bi - br) * root),
        (ci, -cr),
        ((di - dr) * root, (dr + di) * -root),
    ]
    low = [(e[0] + t[0], e[1] + t[1]) for e, t in zip(even, turned)]
    high = [(e[0] - t[0], e[1] - t[1]) for e, t in zip(even, turned)]
    return low + high


def swap(x):
    return [(i, r) for r, i in x]


def turn(x, power):
    power = power % BLOCKS
    if power == 0:
        return x
    c = math.cos(2 * math.pi * power / BLOCKS)
    s = -math.sin(2 * math.pi * power / BLOCKS)
    return (x[0] * c - x[1] * s, x[0] * s + x[1] * c)


def high(a, b, dims=((1,), (0,))):
    return lax.dot_general(
        a, b, (dims, ((), ())), precision=lax.Precision.HIGHEST, preferred_element_type=F32
    )


def kernel(
    a_hbm, inc_hbm, taper, first, twist, back, again, out,
    a_in, inc_in, snd, rcv, incb, incf, lines, weights, spec, mid, pout,
    rs_snd, rs_rcv, qb, fr, fin,
    load_sem, inc_send, inc_recv, incx_send, incx_recv, main_send, main_recv,
    rs_send, rs_recv, ret_send, ret_recv, fin_send, fin_recv,
):
    lon, mem = lax.axis_index("lon"), lax.axis_index("mem")
    z, y, k = lon // 8, (lon // 2) % 4, lon % 2
    zhi, x = mem // XS, mem % XS

    load_a = pltpu.make_async_copy(a_hbm, a_in, load_sem.at[0])
    load_i = pltpu.make_async_copy(inc_hbm, inc_in, load_sem.at[1])
    load_a.start()
    load_i.start()

    def peer(s):
        return ((z + s // 8) % 4) * 8 + ((y + (s // 2) % 4) % 4) * 2 + (k + s % 2) % 2

    barrier = pltpu.get_barrier_semaphore()

    @pl.loop(1, LONS)
    def _(s):
        pl.semaphore_signal(
            barrier, inc=1, device_id={"lon": peer(s), "mem": mem}, device_id_type=MESH
        )

    @pl.loop(0, LONS)
    def _(s):
        there = ((zhi + 1) % 2) * XS + x
        pl.semaphore_signal(
            barrier, inc=1, device_id={"lon": peer(s), "mem": there}, device_id_type=MESH
        )

    @pl.loop(1, XS)
    def _(s):
        there = zhi * XS + (x + s) % XS
        pl.semaphore_signal(
            barrier, inc=1, device_id={"lon": lon, "mem": there}, device_id_type=MESH
        )

    load_a.wait()

    @pl.loop(0, LONS)
    def _(t):
        for pair in range(PAIRS):
            one = a_in[2 * pair, pl.ds(t * LATS, LATS), :].astype(F32)
            two = a_in[2 * pair + 1, pl.ds(t * LATS, LATS), :].astype(F32)
            for c in range(CHUNKS):
                both = jnp.concatenate([one[c * PER : (c + 1) * PER], two[c * PER : (c + 1) * PER]])
                snd[c, t, pl.ds(pair * 16, 16), :] = both.astype(BF16)

    load_i.wait()
    pl.semaphore_wait(barrier, 2 * LONS - 1 + XS - 1)

    @pl.when(lon % XS == x)
    def _():
        @pl.loop(1, LONS)
        def _(s):
            there = peer(s)
            pltpu.make_async_remote_copy(
                src_ref=inc_in.at[pl.ds(there * LATS, LATS)], dst_ref=incb.at[x, lon // XS],
                send_sem=inc_send, recv_sem=inc_recv,
                device_id={"lon": there, "mem": mem}, device_id_type=MESH,
            ).start()

        pltpu.make_async_copy(
            inc_in.at[pl.ds(lon * LATS, LATS)], incb.at[x, lon // XS], inc_recv
        ).start()

    for c in range(CHUNKS):
        @pl.loop(1, LONS)
        def _(s):
            there = peer(s)
            pltpu.make_async_remote_copy(
                src_ref=snd.at[c, there], dst_ref=rcv.at[c, lon],
                send_sem=main_send.at[c], recv_sem=main_recv.at[c],
                device_id={"lon": there, "mem": mem}, device_id_type=MESH,
            ).start()

        pltpu.make_async_copy(snd.at[c, lon], rcv.at[c, lon], main_recv.at[c]).start()

    u = high(first[...], taper[...])
    ur, ui = u[:WIDE], u[WIDE:]
    vr = ur * twist[0] - ui * twist[1]
    vi = ur * twist[1] + ui * twist[0]
    line = high(back[0], vr, ((1,), (1,))) - high(back[1], vi, ((1,), (1,)))
    lines[0, :, :WIDE] = high(again[0], line)
    lines[1, :, :WIDE] = high(again[1], line)
    lines[0, :, WIDE:] = high(again[2], line)
    lines[1, :, WIDE:] = high(again[3], line)

    @pl.loop(0, HALF + 1)
    def _(f):
        def toeplitz(part):
            row = jnp.broadcast_to(lines[part, pl.ds(f, 1), :], (WIDE, 2 * WIDE))
            return pltpu.roll(row, 0, 1, stride=1, stride_axis=0)[:, :WIDE]

        real, imag = toeplitz(0), toeplitz(1)
        weights[f, :WIDE, :WIDE] = real.astype(BF16)
        weights[f, WIDE:, WIDE:] = real.astype(BF16)
        weights[f, :WIDE, WIDE:] = imag.astype(BF16)
        weights[f, WIDE:, :WIDE] = (-imag).astype(BF16)

    pltpu.make_async_copy(incb.at[x], incb.at[x], inc_recv).wait()

    @pl.loop(1, XS)
    def _(s):
        there = zhi * XS + (x + s) % XS
        pltpu.make_async_remote_copy(
            src_ref=incb.at[x], dst_ref=incb.at[x], send_sem=incx_send, recv_sem=incx_recv,
            device_id={"lon": lon, "mem": there}, device_id_type=MESH,
        ).start()

    three = pl.ds(0, XS - 1)
    pltpu.make_async_copy(incb.at[three], incb.at[three], incx_recv).wait()

    @pl.loop(0, LONS)
    def _(i):
        incf[i] = incb[i % XS, i // XS].astype(F32)

    def tile(c, q, n):
        return rcv[c, n // 2, pl.ds(q * 16, 16), (n % 2) * WIDE : (n % 2 + 1) * WIDE].astype(F32)

    for c in range(CHUNKS):
        pltpu.make_async_copy(rcv.at[c], rcv.at[c], main_recv.at[c]).wait()

        @pl.loop(0, PAIRS)
        def _(q):
            for n2 in range(8):
                points = []
                for n1 in range(8):
                    n = 8 * n1 + n2
                    both = tile(c, q, n)
                    field = incf[n // 2, c * PER : (c + 1) * PER, (n % 2) * WIDE : (n % 2 + 1) * WIDE]
                    real = (both[:8] * field).astype(BF16).astype(F32)
                    imag = (both[8:] * field).astype(BF16).astype(F32)
                    points.append((real, imag))
                for f1, value in enumerate(dft8(points)):
                    value = turn(value, n2 * f1)
                    mid[f1 * 8 + n2, 0] = value[0]
                    mid[f1 * 8 + n2, 1] = value[1]
            for f1 in range(8):
                points = [(mid[f1 * 8 + n2, 0], mid[f1 * 8 + n2, 1]) for n2 in range(8)]
                for f2, value in enumerate(dft8(points)):
                    f = f1 + 8 * f2
                    spec[f, pl.ds(q * 8, 8), :WIDE] = value[0]
                    spec[f, pl.ds(q * 8, 8), WIDE:] = value[1] if f <= HALF else -value[1]

        for f in range(HALF + 1):
            if f in (0, HALF):
                spec[f] = jnp.dot(spec[f].astype(BF16), weights[f], preferred_element_type=F32)
            else:
                both = jnp.concatenate([spec[f], spec[BLOCKS - f]]).astype(BF16)
                both = jnp.dot(both, weights[f], preferred_element_type=F32)
                spec[f] = both[: ROWS // 2]
                spec[BLOCKS - f] = both[ROWS // 2 :]

        pout[...] = jnp.zeros_like(pout)

        @pl.loop(0, PAIRS)
        def _(q):
            for f1 in range(8):
                points = []
                for f2 in range(8):
                    f = f1 + 8 * f2
                    real = spec[f, pl.ds(q * 8, 8), :WIDE]
                    imag = spec[f, pl.ds(q * 8, 8), WIDE:]
                    points.append((real, imag if f <= HALF else -imag))
                for n2, value in enumerate(swap(dft8(swap(points)))):
                    value = turn(value, -n2 * f1)
                    mid[n2 * 8 + f1, 0] = value[0]
                    mid[n2 * 8 + f1, 1] = value[1]
            for n2 in range(8):
                points = [(mid[n2 * 8 + f1, 0], mid[n2 * 8 + f1, 1]) for f1 in range(8)]
                for n1, value in enumerate(swap(dft8(swap(points)))):
                    n = 8 * n1 + n2
                    both = tile(c, q, n)
                    pout[n] += value[0] * both[:8] + value[1] * both[8:]

        @pl.loop(0, BLOCKS)
        def _(n):
            whole = pout[n]
            for s in range(XS):
                rs_snd[c, s, n] = whole[2 * s : 2 * s + 2]

        @pl.loop(1, XS)
        def _(s):
            there = (x + s) % XS
            pltpu.make_async_remote_copy(
                src_ref=rs_snd.at[c, there], dst_ref=rs_rcv.at[c, s - 1],
                send_sem=rs_send.at[c], recv_sem=rs_recv.at[c],
                device_id={"lon": lon, "mem": zhi * XS + there}, device_id_type=MESH,
            ).start()

        pltpu.make_async_copy(rs_rcv.at[c], rs_rcv.at[c], rs_recv.at[c]).wait()
        qb[c] = rs_snd[c, x] + rs_rcv[c, 0] + rs_rcv[c, 1] + rs_rcv[c, 2]

        for e in range(2):
            @pl.loop(1 - e, LONS)
            def _(s):
                there = peer(s)
                pltpu.make_async_remote_copy(
                    src_ref=qb.at[c, pl.ds(2 * there, 2)], dst_ref=fr.at[c, zhi, lon],
                    send_sem=ret_send.at[c], recv_sem=ret_recv.at[c],
                    device_id={"lon": there, "mem": ((zhi + e) % 2) * XS + x}, device_id_type=MESH,
                ).start()

        pltpu.make_async_copy(
            qb.at[c, pl.ds(2 * lon, 2)], fr.at[c, zhi, lon], ret_recv.at[c]
        ).start()
        pltpu.make_async_copy(fr.at[c], fr.at[c], ret_recv.at[c]).wait()
        fin[c, x] = fr[c, 0] + fr[c, 1]

        @pl.loop(1, XS)
        def _(s):
            there = zhi * XS + (x + s) % XS
            pltpu.make_async_remote_copy(
                src_ref=fin.at[c, x], dst_ref=fin.at[c, x],
                send_sem=fin_send.at[c], recv_sem=fin_recv.at[c],
                device_id={"lon": lon, "mem": there}, device_id_type=MESH,
            ).start()

    for c in range(CHUNKS):
        pltpu.make_async_copy(fin.at[c, three], fin.at[c, three], fin_recv.at[c]).wait()
        for s in range(XS):
            row = c * PER + 2 * s
            out[:, row : row + 2, :WIDE] = fin[c, s, :, 0]
            out[:, row : row + 2, WIDE:] = fin[c, s, :, 1]

    @pl.when(lon % XS == x)
    def _():
        sent = inc_in.at[pl.ds(0, (LONS - 1) * LATS)]
        pltpu.make_async_copy(sent, sent, inc_send).wait()

    pltpu.make_async_copy(incb.at[three], incb.at[three], incx_send).wait()
    for c in range(CHUNKS):
        sent = snd.at[c, pl.ds(0, LONS - 1)]
        pltpu.make_async_copy(sent, sent, main_send.at[c]).wait()
        pltpu.make_async_copy(rs_rcv.at[c], rs_rcv.at[c], rs_send.at[c]).wait()
        sent = fr.at[c, 0]
        pltpu.make_async_copy(sent, sent, ret_send.at[c]).wait()
        sent = fr.at[c, 0, pl.ds(0, LONS - 1)]
        pltpu.make_async_copy(sent, sent, ret_send.at[c]).wait()
        pltpu.make_async_copy(fin.at[c, three], fin.at[c, three], fin_send.at[c]).wait()


def per_device(anomalies, increment, spectral_taper):
    any_space, vmem = pl.BlockSpec(memory_space=pl.ANY), pl.BlockSpec(memory_space=pltpu.VMEM)
    dma = pltpu.SemaphoreType.DMA
    both = (2 * LONS, 2, WIDE)
    total = pl.pallas_call(
        kernel,
        out_shape=jax.ShapeDtypeStruct((LONS, LATS, 2 * WIDE), F32),
        in_specs=[any_space, any_space] + [vmem] * 5,
        out_specs=vmem,
        scratch_shapes=[
            pltpu.VMEM((MEMBERS, LONS * LATS, 2 * WIDE), BF16),
            pltpu.VMEM((LONS * LATS, 2 * WIDE), BF16),
            pltpu.VMEM((CHUNKS, LONS, ROWS, 2 * WIDE), BF16),
            pltpu.VMEM((CHUNKS, LONS, ROWS, 2 * WIDE), BF16),
            pltpu.VMEM((XS, LONS // XS, LATS, 2 * WIDE), BF16),
            pltpu.VMEM((LONS, LATS, 2 * WIDE), F32),
            pltpu.VMEM((2, 40, 2 * WIDE), F32),
            pltpu.VMEM((HALF + 1, 2 * WIDE, 2 * WIDE), BF16),
            pltpu.VMEM((BLOCKS, ROWS // 2, 2 * WIDE), F32),
            pltpu.VMEM((BLOCKS, 2, 8, WIDE), F32),
            pltpu.VMEM((BLOCKS, PER, WIDE), F32),
            pltpu.VMEM((CHUNKS, XS) + both, F32),
            pltpu.VMEM((CHUNKS, XS - 1) + both, F32),
            pltpu.VMEM((CHUNKS,) + both, F32),
            pltpu.VMEM((CHUNKS, 2, LONS, 2, 2, WIDE), F32),
            pltpu.VMEM((CHUNKS, XS, LONS, 2, 2, WIDE), F32),
            dma((2,)), dma, dma, dma, dma, dma((CHUNKS,)), dma((CHUNKS,)),
            dma((CHUNKS,)), dma((CHUNKS,)), dma((CHUNKS,)), dma((CHUNKS,)),
            dma((CHUNKS,)), dma((CHUNKS,)),
        ],
        compiler_params=pltpu.CompilerParams(
            collective_id=0, has_side_effects=True, vmem_limit_bytes=48 << 20
        ),
        name="localize",
    )(anomalies, increment, spectral_taper.reshape(BLOCKS, WIDE), *tables())
    members = lax.axis_size("mem") * MEMBERS
    return total.reshape(LONS * LATS, 2 * WIDE) / (members - 1)


def solution(mesh):
    in_specs = (P("mem", None, "lon"), P(None, "lon"), P())
    return jax.shard_map(
        per_device, mesh=mesh, in_specs=in_specs, out_specs=P(None, "lon"), check_vma=False
    )
```

```python
import functools
import math

import jax
import jax.numpy as jnp
import numpy as np
from jax import lax
from jax.experimental import pallas as pl
from jax.experimental.pallas import tpu as pltpu
from jax.sharding import PartitionSpec as P

MESH = pl.DeviceIdType.MESH
NLON = 8192
BLOCKS = 64
WIDE = 128
HALF = BLOCKS // 2
LONS = 32
XS = 4
LATS = 16
CHUNKS = 4
AHEAD = 2
MIXED = 2
PER = LATS // CHUNKS
MEMBERS = 8
ROWS = PER * MEMBERS
PAIRS = ROWS // 16
F32 = jnp.float32
BF16 = jnp.bfloat16


def tables():
    s = np.arange(WIDE)[:, None]
    r = np.arange(BLOCKS)[None, :]
    first = 2 * math.pi * (s * r % BLOCKS) / BLOCKS
    first = np.concatenate([np.cos(first), np.sin(first)], 0)
    c = np.arange(WIDE)[None, :]
    twist = 2 * math.pi * (s * c % NLON) / NLON
    twist = np.stack([np.cos(twist), np.sin(twist)])
    d = np.arange(BLOCKS)[:, None]
    back = 2 * math.pi * (d * c % BLOCKS) / BLOCKS
    back = np.stack([np.cos(back), np.sin(back)]) / (NLON * BLOCKS)
    f = np.arange(40)[:, None]
    d = np.arange(BLOCKS)[None, :]
    here = 2 * math.pi * (f * d % BLOCKS) / BLOCKS
    there = 2 * math.pi * (f * (d + 1) % BLOCKS) / BLOCKS
    again = np.stack([np.cos(here), -np.sin(here), np.cos(there), -np.sin(there)])
    return [np.asarray(t, np.float32) for t in (first, twist, back, again)]


def dft4(x):
    (ar, ai), (br, bi), (cr, ci), (dr, di) = x
    er, ei, fr, fi = ar + cr, ai + ci, ar - cr, ai - ci
    gr, gi, hr, hi = br + dr, bi + di, br - dr, bi - di
    return [(er + gr, ei + gi), (fr + hi, fi - hr), (er - gr, ei - gi), (fr - hi, fi + hr)]


def dft8(x):
    even, odd = dft4(x[0::2]), dft4(x[1::2])
    root = math.sqrt(0.5)
    (ar, ai), (br, bi), (cr, ci), (dr, di) = odd
    turned = [
        (ar, ai),
        ((br + bi) * root, (bi - br) * root),
        (ci, -cr),
        ((di - dr) * root, (dr + di) * -root),
    ]
    low = [(e[0] + t[0], e[1] + t[1]) for e, t in zip(even, turned)]
    high = [(e[0] - t[0], e[1] - t[1]) for e, t in zip(even, turned)]
    return low + high


def swap(x):
    return [(i, r) for r, i in x]


def turn(x, power):
    power = power % BLOCKS
    if power == 0:
        return x
    c = math.cos(2 * math.pi * power / BLOCKS)
    s = -math.sin(2 * math.pi * power / BLOCKS)
    return (x[0] * c - x[1] * s, x[0] * s + x[1] * c)


def high(a, b, dims=((1,), (0,))):
    return lax.dot_general(
        a, b, (dims, ((), ())), precision=lax.Precision.HIGHEST, preferred_element_type=F32
    )


def kernel(
    a_hbm, inc_hbm, taper_hbm, first_hbm, twist_hbm, back_hbm, again_hbm, out,
    a_in, inc_in, taper, first, twist, back, again,
    snd, rcv, xsnd, xrcv, incb, incf, lines, weights, spec, mid, pout, rs_snd, rs_rcv, qb, fr, part, fin,
    load_sem, inc_send, inc_recv, incx_send, incx_recv, main_send, main_recv,
    x_send, x_recv, rs_send, rs_recv, ret_send, ret_recv, fin_send, fin_recv, group_sem,
):
    lon, mem = lax.axis_index("lon"), lax.axis_index("mem")
    z, y, k = lon // 8, (lon // 2) % 4, lon % 2
    zhi, x = mem // XS, mem % XS

    def load(source, target, sem):
        copy = pltpu.make_async_copy(source, target, load_sem.at[sem])
        copy.start()
        return copy

    load_a = [load(a_hbm.at[j], a_in.at[j], j) for j in range(MEMBERS)]
    load_i = load(inc_hbm, inc_in, MEMBERS)
    pairs = [(taper_hbm, taper), (first_hbm, first), (twist_hbm, twist), (back_hbm, back), (again_hbm, again)]
    load_t = [load(a, b, MEMBERS + 1 + i) for i, (a, b) in enumerate(pairs)]

    def after(v, d):
        return (v + d) % 4

    zs = [after(z, d) * 8 for d in range(4)]
    ys = [after(y, d) * 2 for d in range(4)]
    ks = [k, 1 - k]
    peers = [zs[s // 8] + ys[s // 2 % 4] + ks[s % 2] for s in range(LONS)]
    xs = [(x + d) % XS for d in range(XS)]
    mems = [zhi * XS + xs[d] for d in range(XS)]
    groups = [mem, (1 - zhi) * XS + x]
    rows16 = [zs[s // 2] + ys[0] + ks[s % 2] for s in range(8)]

    barrier = pltpu.get_barrier_semaphore()

    def greet(there, group):
        pl.semaphore_signal(
            barrier, inc=1, device_id={"lon": there, "mem": group}, device_id_type=MESH
        )

    for s in range(1, LONS):
        greet(peers[s], mem)
    greet(lon, groups[1])
    for d in range(1, XS):
        greet(lon, mems[d])

    def remote(source, target, send, recv, there, group):
        pltpu.make_async_remote_copy(
            src_ref=source, dst_ref=target, send_sem=send, recv_sem=recv,
            device_id={"lon": there, "mem": group}, device_id_type=MESH,
        ).start()

    def local(source, target, sem):
        pltpu.make_async_copy(source, target, sem).start()

    def done(ref, sem):
        pltpu.make_async_copy(ref, ref, sem).wait()

    wanted = lax.broadcasted_iota(jnp.int32, (8, WIDE), 0)
    upper = wanted < PER

    def rearrange(c):
        half, low = c // 2, c % 2 == 0

        @pl.loop(0, LONS)
        def _(t):
            for w in range(2):
                cols = slice(w * WIDE, (w + 1) * WIDE)
                parts = []
                for j in range(MEMBERS):
                    whole = a_in[j, pl.ds(t * LATS, LATS), cols].astype(F32)
                    parts.append(whole[half * 8 : half * 8 + 8])
                for j in range(0, MEMBERS, 4):
                    rows = []
                    for i in (j, j + 2):
                        one, two = parts[i], parts[i + 1]
                        if low:
                            two = pltpu.roll(two, PER, 0)
                        else:
                            one = pltpu.roll(one, PER, 0)
                        rows.append(jnp.where(upper, one, two))
                    snd[c, t, pl.ds(j * PER, 4 * PER), cols] = jnp.concatenate(rows).astype(BF16)

    def gather_x():
        row = lax.broadcasted_iota(jnp.int32, (XS * MEMBERS, MEMBERS * LATS), 0)
        col = lax.broadcasted_iota(jnp.int32, (XS * MEMBERS, MEMBERS * LATS), 1)
        for c in range(MIXED, CHUNKS):
            pick = (col == row % MEMBERS * LATS + c * PER + row // MEMBERS).astype(BF16)

            @pl.loop(0, LONS // 2)
            def _(u):
                picked = []
                for e in range(2):
                    whole = a_in[:, pl.ds((2 * u + e) * LATS, LATS), :]
                    whole = whole.reshape(MEMBERS * LATS, 2 * WIDE)
                    picked.append(jnp.dot(pick, whole, preferred_element_type=F32))
                for s in range(XS):
                    both = [p[s * MEMBERS : (s + 1) * MEMBERS] for p in picked]
                    xsnd[c - MIXED, s, u] = jnp.concatenate(both).astype(BF16)

    def send_x(c):
        m = c - MIXED
        for d in range(1, XS):
            remote(xsnd.at[m, xs[d]], xrcv.at[m, x], x_send.at[m], x_recv.at[m], lon, mems[d])
        local(xsnd.at[m, x], xrcv.at[m, x], x_recv.at[m])

    def rearrange_mixed(c):
        m = c - MIXED
        done(xrcv.at[m], x_recv.at[m])

        @pl.loop(0, LONS // 2)
        def _(u):
            for s in range(0, XS, 2):
                one, two = xrcv[m, s, u].astype(F32), xrcv[m, s + 1, u].astype(F32)
                for e in range(2):
                    both = [v[e * MEMBERS : (e + 1) * MEMBERS] for v in (one, two)]
                    snd[c, 2 * u + e, s * MEMBERS : (s + 2) * MEMBERS] = jnp.concatenate(both).astype(BF16)

    def send_main(c):
        for s in range(1, LONS):
            remote(snd.at[c, peers[s]], rcv.at[c, lon], main_send.at[c], main_recv.at[c], peers[s], mem)
        local(snd.at[c, lon], rcv.at[c, lon], main_recv.at[c])

    for copy in load_a:
        copy.wait()
    rearrange(0)
    load_i.wait()
    pl.semaphore_wait(barrier, LONS + XS - 1)
    pl.semaphore_signal(
        group_sem, inc=1, device_id={"lon": lon, "mem": groups[1]}, device_id_type=MESH
    )

    @pl.when(lon % XS == x)
    def _():
        for s in range(1, LONS):
            block = inc_in.at[pl.ds(peers[s] * LATS, LATS)]
            remote(block, incb.at[x, lon // XS], inc_send, inc_recv, peers[s], mem)
        local(inc_in.at[pl.ds(lon * LATS, LATS)], incb.at[x, lon // XS], inc_recv)

    send_main(0)
    gather_x()
    for c in range(MIXED, CHUNKS):
        send_x(c)
    for c in range(1, MIXED):
        rearrange(c)
        if c < AHEAD:
            send_main(c)
    for c in range(MIXED, AHEAD):
        rearrange_mixed(c)
        send_main(c)

    for copy in load_t:
        copy.wait()

    u = high(first[...], taper[...])
    ur, ui = u[:WIDE], u[WIDE:]
    vr = ur * twist[0] - ui * twist[1]
    vi = ur * twist[1] + ui * twist[0]
    line = high(back[0], vr, ((1,), (1,))) - high(back[1], vi, ((1,), (1,)))
    lines[0, :, :WIDE] = high(again[0], line)
    lines[1, :, :WIDE] = high(again[1], line)
    lines[0, :, WIDE:] = high(again[2], line)
    lines[1, :, WIDE:] = high(again[3], line)

    @pl.loop(0, HALF + 1)
    def _(f):
        def toeplitz(part):
            row = jnp.broadcast_to(lines[part, pl.ds(f, 1), :], (WIDE, 2 * WIDE))
            return pltpu.roll(row, 0, 1, stride=1, stride_axis=0)[:, :WIDE]

        real, imag = toeplitz(0), toeplitz(1)
        weights[f, :WIDE, :WIDE] = real.astype(BF16)
        weights[f, WIDE:, WIDE:] = real.astype(BF16)
        weights[f, :WIDE, WIDE:] = imag.astype(BF16)
        weights[f, WIDE:, :WIDE] = (-imag).astype(BF16)

    done(incb.at[x], inc_recv)
    for d in range(1, XS):
        remote(incb.at[x], incb.at[x], incx_send, incx_recv, lon, mems[d])
    three = pl.ds(0, XS - 1)
    done(incb.at[three], incx_recv)

    @pl.loop(0, LONS)
    def _(i):
        for w in range(2):
            whole = incb[i % XS, i // XS, :, w * WIDE : (w + 1) * WIDE].astype(F32)
            for c in range(CHUNKS):
                part = whole[c // 2 * 8 : c // 2 * 8 + 8]
                turned = pltpu.roll(part, PER, 0)
                one, two = (part, turned) if c % 2 == 0 else (turned, part)
                if c < MIXED:
                    incf[c, 2 * i + w] = jnp.where(upper, one, two)
                else:
                    mine = jnp.where(wanted == c % 2 * PER + x, part, 0.0)
                    mine = jnp.sum(mine, axis=0, keepdims=True)
                    incf[c, 2 * i + w] = jnp.broadcast_to(mine, (8, WIDE))

    def tile(c, q, n):
        return rcv[c, n // 2, pl.ds(q * 16, 16), (n % 2) * WIDE : (n % 2 + 1) * WIDE].astype(F32)

    def convolve(c):
        @pl.loop(0, PAIRS)
        def _(q):
            for n2 in range(8):
                points = []
                for n1 in range(8):
                    n = 8 * n1 + n2
                    both = tile(c, q, n)
                    field = incf[c, n]
                    real = (both[:8] * field).astype(BF16).astype(F32)
                    imag = (both[8:] * field).astype(BF16).astype(F32)
                    points.append((real, imag))
                for f1, value in enumerate(dft8(points)):
                    value = turn(value, n2 * f1)
                    mid[f1 * 8 + n2, 0] = value[0]
                    mid[f1 * 8 + n2, 1] = value[1]
            for f1 in range(8):
                points = [(mid[f1 * 8 + n2, 0], mid[f1 * 8 + n2, 1]) for n2 in range(8)]
                for f2, value in enumerate(dft8(points)):
                    f = f1 + 8 * f2
                    spec[f, pl.ds(q * 8, 8), :WIDE] = value[0]
                    spec[f, pl.ds(q * 8, 8), WIDE:] = value[1] if f <= HALF else -value[1]
            pass

        for f in range(HALF + 1):
            if f in (0, HALF):
                spec[f] = jnp.dot(spec[f].astype(BF16), weights[f], preferred_element_type=F32)
            else:
                both = jnp.concatenate([spec[f], spec[BLOCKS - f]]).astype(BF16)
                both = jnp.dot(both, weights[f], preferred_element_type=F32)
                spec[f] = both[: ROWS // 2]
                spec[BLOCKS - f] = both[ROWS // 2 :]

        pout[...] = jnp.zeros_like(pout)

        @pl.loop(0, PAIRS)
        def _(q):
            for f1 in range(8):
                points = []
                for f2 in range(8):
                    f = f1 + 8 * f2
                    real = spec[f, pl.ds(q * 8, 8), :WIDE]
                    imag = spec[f, pl.ds(q * 8, 8), WIDE:]
                    points.append((real, imag if f <= HALF else -imag))
                for n2, value in enumerate(swap(dft8(swap(points)))):
                    value = turn(value, -n2 * f1)
                    mid[n2 * 8 + f1, 0] = value[0]
                    mid[n2 * 8 + f1, 1] = value[1]
            for n2 in range(8):
                points = [(mid[n2 * 8 + f1, 0], mid[n2 * 8 + f1, 1]) for f1 in range(8)]
                for n1, value in enumerate(swap(dft8(swap(points)))):
                    n = 8 * n1 + n2
                    both = tile(c, q, n)
                    pout[n] += value[0] * both[:8] + value[1] * both[8:]
            pass

        @pl.loop(0, BLOCKS // 2)
        def _(i):
            zk, row = i // 8 * 2 + i % 2, i // 2 % 4
            for w in range(2):
                whole = pout[2 * i + w]
                whole = whole + pltpu.roll(whole, 4, 0)
                if c < MIXED:
                    for s in range(XS):
                        rs_snd[c, s, zk, row, w : w + 1] = whole[s : s + 1]
                else:
                    whole = whole + pltpu.roll(whole, 2, 0)
                    whole = whole + pltpu.roll(whole, 1, 0)
                    qb[c, zk, row, w : w + 1] = whole[:1]

    def send_sums(c):
        for d in range(1, XS):
            remote(rs_snd.at[c, xs[d]], rs_rcv.at[c, d - 1], rs_send.at[c], rs_recv.at[c], lon, mems[d])

    def send_back(c):
        if c < MIXED:
            done(rs_rcv.at[c], rs_recv.at[c])
            qb[c] = rs_snd[c, x] + rs_rcv[c, 0] + rs_rcv[c, 1] + rs_rcv[c, 2]
        for g in (1, 0):
            for s in range(8):
                if g or s:
                    index = zs[s // 2] // 4 + ks[s % 2]
                    remote(
                        qb.at[c, index], fr.at[c, zhi, z * 2 + k], ret_send.at[c], ret_recv.at[c],
                        rows16[s], groups[g],
                    )
        local(qb.at[c, z * 2 + k], fr.at[c, zhi, z * 2 + k], ret_recv.at[c])

    def send_all(c):
        done(fr.at[c], ret_recv.at[c])
        for row in range(4):
            part[c, row] = fr[c, 0, :, row] + fr[c, 1, :, row]
        for d in (2, 1, 3, 0):
            for e in (2, 1, 3, 0):
                if d or e:
                    there = z * 8 + ys[e] + k
                    remote(part.at[c, ys[e] // 2], fin.at[c, x, y], fin_send.at[c], fin_recv.at[c], there, mems[d])
        local(part.at[c, y], fin.at[c, x, y], fin_recv.at[c])

    def assemble(c):
        done(fin.at[c], fin_recv.at[c])

        @pl.loop(0, 4)
        def _(row):
            for s in range(XS):
                for i in range(8):
                    at = c * PER + s
                    out[i // 2 * 8 + row * 2 + i % 2, at : at + 1, :WIDE] = fin[c, s, row, i, 0:1]
                    out[i // 2 * 8 + row * 2 + i % 2, at : at + 1, WIDE:] = fin[c, s, row, i, 1:2]

    for step in range(CHUNKS):
        done(rcv.at[step], main_recv.at[step])
        later = step + AHEAD
        if later < CHUNKS:
            if later >= MIXED:
                rearrange_mixed(later)
            send_main(later)
        convolve(step)
        if step == 0:
            pl.semaphore_wait(group_sem, 1)
        if step < MIXED:
            send_sums(step)
        else:
            send_back(step)
        if 1 <= step <= MIXED:
            send_back(step - 1)
        if step >= 2:
            send_all(step - 2)

    for c in range(CHUNKS - 2, CHUNKS):
        if c == MIXED - 1 == CHUNKS - 1:
            send_back(c)
        send_all(c)
    for c in range(CHUNKS):
        assemble(c)

    @pl.when(lon % XS == x)
    def _():
        done(inc_in.at[pl.ds(0, (LONS - 1) * LATS)], inc_send)

    done(incb.at[three], incx_send)
    for c in range(CHUNKS):
        done(snd.at[c, pl.ds(0, LONS - 1)], main_send.at[c])
        if c >= MIXED:
            done(xsnd.at[c - MIXED, three], x_send.at[c - MIXED])
        if c < MIXED:
            done(rs_rcv.at[c], rs_send.at[c])
        done(fr.at[c, 0], ret_send.at[c])
        done(fr.at[c, 0, pl.ds(0, 7)], ret_send.at[c])
        done(fin.at[c, 0], fin_send.at[c])
        done(fin.at[c, 1], fin_send.at[c])
        done(fin.at[c, 2], fin_send.at[c])
        done(fin.at[c, 0, pl.ds(0, 3)], fin_send.at[c])


def per_device(anomalies, increment, spectral_taper):
    hbm, vmem = pl.BlockSpec(memory_space=pltpu.HBM), pl.BlockSpec(memory_space=pltpu.VMEM)
    constants = tables()
    dma = pltpu.SemaphoreType.DMA
    circle = (8, 4, 2, WIDE)
    mixed = (max(CHUNKS - MIXED, 1), XS, LONS // 2, 2 * MEMBERS, 2 * WIDE)
    total = pl.pallas_call(
        kernel,
        out_shape=jax.ShapeDtypeStruct((LONS, LATS, 2 * WIDE), F32),
        in_specs=[hbm] * 7,
        out_specs=vmem,
        scratch_shapes=[
            pltpu.VMEM((MEMBERS, LONS * LATS, 2 * WIDE), BF16),
            pltpu.VMEM((LONS * LATS, 2 * WIDE), BF16),
            pltpu.VMEM((BLOCKS, WIDE), F32),
        ]
        + [pltpu.VMEM(t.shape, F32) for t in constants]
        + [
            pltpu.VMEM((CHUNKS, LONS, ROWS, 2 * WIDE), BF16),
            pltpu.VMEM((CHUNKS, LONS, ROWS, 2 * WIDE), BF16),
            pltpu.VMEM(mixed, BF16),
            pltpu.VMEM(mixed, BF16),
            pltpu.VMEM((XS, LONS // XS, LATS, 2 * WIDE), BF16),
            pltpu.VMEM((CHUNKS, BLOCKS, 8, WIDE), F32),
            pltpu.VMEM((2, 40, 2 * WIDE), F32),
            pltpu.VMEM((HALF + 1, 2 * WIDE, 2 * WIDE), BF16),
            pltpu.VMEM((BLOCKS, ROWS // 2, 2 * WIDE), F32),
            pltpu.VMEM((BLOCKS, 2, 8, WIDE), F32),
            pltpu.VMEM((BLOCKS, 8, WIDE), F32),
            pltpu.VMEM((CHUNKS, XS) + circle, F32),
            pltpu.VMEM((CHUNKS, XS - 1) + circle, F32),
            pltpu.VMEM((CHUNKS,) + circle, F32),
            pltpu.VMEM((CHUNKS, 2) + circle, F32),
            pltpu.VMEM((CHUNKS, 4, 8, 2, WIDE), F32),
            pltpu.VMEM((CHUNKS, XS, 4, 8, 2, WIDE), F32),
            dma((MEMBERS + 6,)), dma, dma, dma, dma, dma((CHUNKS,)), dma((CHUNKS,)),
            dma((CHUNKS,)), dma((CHUNKS,)), dma((CHUNKS,)), dma((CHUNKS,)), dma((CHUNKS,)), dma((CHUNKS,)),
            dma((CHUNKS,)), dma((CHUNKS,)), pltpu.SemaphoreType.REGULAR,
        ],
        compiler_params=pltpu.CompilerParams(
            collective_id=0, has_side_effects=True, vmem_limit_bytes=62 << 20
        ),
        name="localize",
    )(anomalies, increment, spectral_taper.reshape(BLOCKS, WIDE), *constants)
    members = lax.axis_size("mem") * MEMBERS
    return total.reshape(LONS * LATS, 2 * WIDE) / (members - 1)


def solution(mesh):
    in_specs = (P("mem", None, "lon"), P(None, "lon"), P())
    return jax.shard_map(
        per_device, mesh=mesh, in_specs=in_specs, out_specs=P(None, "lon"), check_vma=False
    )
```

```python
import functools
import math

import jax
import jax.numpy as jnp
import numpy as np
from jax import lax
from jax.experimental import pallas as pl
from jax.experimental.pallas import tpu as pltpu
from jax.sharding import PartitionSpec as P

MESH = pl.DeviceIdType.MESH
NLON = 8192
BLOCKS = 64
WIDE = 128
HALF = BLOCKS // 2
LONS = 32
XS = 4
LATS = 16
CHUNKS = 4
SETS = ((0, 1), (2,), (3,))
MIXED = 2
PER = LATS // CHUNKS
MEMBERS = 8
ROWS = PER * MEMBERS
PAIRS = ROWS // 16
F32 = jnp.float32
BF16 = jnp.bfloat16


def tables():
    s = np.arange(WIDE)[:, None]
    r = np.arange(BLOCKS)[None, :]
    first = 2 * math.pi * (s * r % BLOCKS) / BLOCKS
    first = np.concatenate([np.cos(first), np.sin(first)], 0)
    c = np.arange(WIDE)[None, :]
    twist = 2 * math.pi * (s * c % NLON) / NLON
    twist = np.stack([np.cos(twist), np.sin(twist)])
    d = np.arange(BLOCKS)[:, None]
    back = 2 * math.pi * (d * c % BLOCKS) / BLOCKS
    back = np.stack([np.cos(back), np.sin(back)]) / (NLON * BLOCKS)
    f = np.arange(40)[:, None]
    d = np.arange(BLOCKS)[None, :]
    here = 2 * math.pi * (f * d % BLOCKS) / BLOCKS
    there = 2 * math.pi * (f * (d + 1) % BLOCKS) / BLOCKS
    again = np.stack([np.cos(here), -np.sin(here), np.cos(there), -np.sin(there)])
    return [np.asarray(t, np.float32) for t in (first, twist, back, again)]


def dft4(x):
    (ar, ai), (br, bi), (cr, ci), (dr, di) = x
    er, ei, fr, fi = ar + cr, ai + ci, ar - cr, ai - ci
    gr, gi, hr, hi = br + dr, bi + di, br - dr, bi - di
    return [(er + gr, ei + gi), (fr + hi, fi - hr), (er - gr, ei - gi), (fr - hi, fi + hr)]


def dft8(x):
    even, odd = dft4(x[0::2]), dft4(x[1::2])
    root = math.sqrt(0.5)
    (ar, ai), (br, bi), (cr, ci), (dr, di) = odd
    turned = [
        (ar, ai),
        ((br + bi) * root, (bi - br) * root),
        (ci, -cr),
        ((di - dr) * root, (dr + di) * -root),
    ]
    low = [(e[0] + t[0], e[1] + t[1]) for e, t in zip(even, turned)]
    high = [(e[0] - t[0], e[1] - t[1]) for e, t in zip(even, turned)]
    return low + high


def swap(x):
    return [(i, r) for r, i in x]


def turn(x, power):
    power = power % BLOCKS
    if power == 0:
        return x
    c = math.cos(2 * math.pi * power / BLOCKS)
    s = -math.sin(2 * math.pi * power / BLOCKS)
    return (x[0] * c - x[1] * s, x[0] * s + x[1] * c)


def high(a, b, dims=((1,), (0,))):
    return lax.dot_general(
        a, b, (dims, ((), ())), precision=lax.Precision.HIGHEST, preferred_element_type=F32
    )


def kernel(
    a_hbm, inc_hbm, taper_hbm, first_hbm, twist_hbm, back_hbm, again_hbm, out,
    a_in, inc_in, taper, first, twist, back, again,
    snd, rcv, xsnd, xrcv, incb, incf, lines, weights, spec, mid, pout, rs_snd, rs_rcv,
    load_sem, inc_send, inc_recv, incx_send, incx_recv, main_send, main_recv,
    x_send, x_recv, rs_send, rs_recv, ret_send, ret_recv, fin_send, fin_recv, group_sem, *sums,
):
    lon, mem = lax.axis_index("lon"), lax.axis_index("mem")
    z, y, k = lon // 8, (lon // 2) % 4, lon % 2
    zhi, x = mem // XS, mem % XS

    qb, fr, part, fin = [sums[i * len(SETS) : (i + 1) * len(SETS)] for i in range(4)]

    def load(source, target, sem):
        copy = pltpu.make_async_copy(source, target, load_sem.at[sem])
        copy.start()
        return copy

    group = MEMBERS // 2
    load_a = [load(a_hbm.at[pl.ds(j * group, group)], a_in.at[pl.ds(j * group, group)], j) for j in range(2)]

    def after(v, d):
        return (v + d) % 4

    zs = [after(z, d) * 8 for d in range(4)]
    ys = [after(y, d) * 2 for d in range(4)]
    ks = [k, 1 - k]
    peers = [zs[s // 8] + ys[s // 2 % 4] + ks[s % 2] for s in range(LONS)]
    xs = [(x + d) % XS for d in range(XS)]
    mems = [zhi * XS + xs[d] for d in range(XS)]
    groups = [mem, (1 - zhi) * XS + x]
    rows16 = [zs[s // 2] + ys[0] + ks[s % 2] for s in range(8)]

    barrier = pltpu.get_barrier_semaphore()

    def greet(there, group):
        pl.semaphore_signal(
            barrier, inc=1, device_id={"lon": there, "mem": group}, device_id_type=MESH
        )

    greet(lon, groups[1])
    for s in reversed(range(1, LONS)):
        greet(peers[s], mem)
    for d in range(1, XS):
        greet(lon, mems[d])

    load_i = load(inc_hbm, inc_in, 2)
    pairs = [(taper_hbm, taper), (first_hbm, first), (twist_hbm, twist), (back_hbm, back), (again_hbm, again)]
    load_t = [load(a, b, 3 + i) for i, (a, b) in enumerate(pairs)]

    def remote(source, target, send, recv, there, group):
        pltpu.make_async_remote_copy(
            src_ref=source, dst_ref=target, send_sem=send, recv_sem=recv,
            device_id={"lon": there, "mem": group}, device_id_type=MESH,
        ).start()

    def local(source, target, sem):
        pltpu.make_async_copy(source, target, sem).start()

    def done(ref, sem):
        pltpu.make_async_copy(ref, ref, sem).wait()

    wanted = lax.broadcasted_iota(jnp.int32, (8, WIDE), 0)
    upper = wanted < PER

    def rearrange(c):
        half, low = c // 2, c % 2 == 0

        @pl.loop(0, LONS)
        def _(t):
            for w in range(2):
                cols = slice(w * WIDE, (w + 1) * WIDE)
                parts = []
                for j in range(MEMBERS):
                    whole = a_in[j, pl.ds(t * LATS, LATS), cols].astype(F32)
                    parts.append(whole[half * 8 : half * 8 + 8])
                for j in range(0, MEMBERS, 4):
                    rows = []
                    for i in (j, j + 2):
                        one, two = parts[i], parts[i + 1]
                        if low:
                            two = pltpu.roll(two, PER, 0)
                        else:
                            one = pltpu.roll(one, PER, 0)
                        rows.append(jnp.where(upper, one, two))
                    snd[c, t, pl.ds(j * PER, 4 * PER), cols] = jnp.concatenate(rows).astype(BF16)

    def gather_x():
        row = lax.broadcasted_iota(jnp.int32, (XS * MEMBERS, MEMBERS * LATS), 0)
        col = lax.broadcasted_iota(jnp.int32, (XS * MEMBERS, MEMBERS * LATS), 1)
        for c in range(MIXED, CHUNKS):
            pick = (col == row % MEMBERS * LATS + c * PER + row // MEMBERS).astype(BF16)

            @pl.loop(0, LONS // 2)
            def _(u):
                picked = []
                for e in range(2):
                    whole = a_in[:, pl.ds((2 * u + e) * LATS, LATS), :]
                    whole = whole.reshape(MEMBERS * LATS, 2 * WIDE)
                    picked.append(jnp.dot(pick, whole, preferred_element_type=F32))
                for s in range(XS):
                    both = [p[s * MEMBERS : (s + 1) * MEMBERS] for p in picked]
                    xsnd[c - MIXED, s, u] = jnp.concatenate(both).astype(BF16)

    def send_x(c):
        m = c - MIXED
        for d in range(1, XS):
            remote(xsnd.at[m, xs[d]], xrcv.at[m, x], x_send.at[m], x_recv.at[m], lon, mems[d])
        local(xsnd.at[m, x], xrcv.at[m, x], x_recv.at[m])

    def rearrange_mixed(c):
        m = c - MIXED
        done(xrcv.at[m], x_recv.at[m])

        @pl.loop(0, LONS // 2)
        def _(u):
            for s in range(0, XS, 2):
                one, two = xrcv[m, s, u].astype(F32), xrcv[m, s + 1, u].astype(F32)
                for e in range(2):
                    both = [v[e * MEMBERS : (e + 1) * MEMBERS] for v in (one, two)]
                    snd[c, 2 * u + e, s * MEMBERS : (s + 2) * MEMBERS] = jnp.concatenate(both).astype(BF16)

    def send_main(c, half):
        for s in range(1, LONS):
            if s % 2 == half:
                remote(snd.at[c, peers[s]], rcv.at[c, lon], main_send.at[c], main_recv.at[c], peers[s], mem)
        if half:
            local(snd.at[c, lon], rcv.at[c, lon], main_recv.at[c])

    for copy in load_a:
        copy.wait()
    rearrange(0)
    load_i.wait()
    pl.semaphore_wait(barrier, LONS + XS - 1)
    pl.semaphore_signal(
        group_sem, inc=1, device_id={"lon": lon, "mem": groups[1]}, device_id_type=MESH
    )

    @pl.when(lon % XS == x)
    def _():
        for s in range(1, LONS):
            block = inc_in.at[pl.ds(peers[s] * LATS, LATS)]
            remote(block, incb.at[x, lon // XS], inc_send, inc_recv, peers[s], mem)
        local(inc_in.at[pl.ds(lon * LATS, LATS)], incb.at[x, lon // XS], inc_recv)

    send_main(0, 0)
    send_main(0, 1)
    for c in range(1, MIXED):
        rearrange(c)
    gather_x()
    done(incb.at[x], inc_recv)
    for d in range(1, XS):
        remote(incb.at[x], incb.at[x], incx_send, incx_recv, lon, mems[d])
    for c in range(MIXED, CHUNKS):
        send_x(c)
    send_main(1, 0)

    for copy in load_t:
        copy.wait()

    u = high(first[...], taper[...])
    ur, ui = u[:WIDE], u[WIDE:]
    vr = ur * twist[0] - ui * twist[1]
    vi = ur * twist[1] + ui * twist[0]
    line = high(back[0], vr, ((1,), (1,))) - high(back[1], vi, ((1,), (1,)))
    lines[0, :, :WIDE] = high(again[0], line)
    lines[1, :, :WIDE] = high(again[1], line)
    lines[0, :, WIDE:] = high(again[2], line)
    lines[1, :, WIDE:] = high(again[3], line)

    @pl.loop(0, HALF + 1)
    def _(f):
        def toeplitz(part):
            row = jnp.broadcast_to(lines[part, pl.ds(f, 1), :], (WIDE, 2 * WIDE))
            return pltpu.roll(row, 0, 1, stride=1, stride_axis=0)[:, :WIDE]

        real, imag = toeplitz(0), toeplitz(1)
        weights[f, :, :WIDE] = real.astype(BF16)
        weights[f, :, WIDE:] = imag.astype(BF16)

    three = pl.ds(0, XS - 1)
    done(incb.at[three], incx_recv)

    @pl.loop(0, LONS)
    def _(i):
        for w in range(2):
            whole = incb[i % XS, i // XS, :, w * WIDE : (w + 1) * WIDE].astype(F32)
            for c in range(CHUNKS):
                part = whole[c // 2 * 8 : c // 2 * 8 + 8]
                turned = pltpu.roll(part, PER, 0)
                one, two = (part, turned) if c % 2 == 0 else (turned, part)
                if c < MIXED:
                    incf[c, 2 * i + w] = jnp.where(upper, one, two)
                else:
                    mine = jnp.where(wanted == c % 2 * PER + x, part, 0.0)
                    mine = jnp.sum(mine, axis=0, keepdims=True)
                    incf[c, 2 * i + w] = jnp.broadcast_to(mine, (8, WIDE))

    def tile(c, q, n):
        return rcv[c, n // 2, pl.ds(q * 16, 16), (n % 2) * WIDE : (n % 2 + 1) * WIDE].astype(F32)

    def convolve(c):
        @pl.loop(0, PAIRS)
        def _(q):
            for n2 in range(8):
                points = []
                for n1 in range(8):
                    n = 8 * n1 + n2
                    both = tile(c, q, n)
                    field = incf[c, n]
                    real = (both[:8] * field).astype(BF16).astype(F32)
                    imag = (both[8:] * field).astype(BF16).astype(F32)
                    points.append((real, imag))
                for f1, value in enumerate(dft8(points)):
                    value = turn(value, n2 * f1)
                    mid[f1 * 8 + n2, 0] = value[0]
                    mid[f1 * 8 + n2, 1] = value[1]
            for f1 in range(8):
                points = [(mid[f1 * 8 + n2, 0], mid[f1 * 8 + n2, 1]) for n2 in range(8)]
                for f2, value in enumerate(dft8(points)):
                    f = f1 + 8 * f2
                    spec[f, pl.ds(q * 8, 8), :WIDE] = value[0]
                    spec[f, pl.ds(q * 8, 8), WIDE:] = value[1] if f <= HALF else -value[1]
            pass

        for f in range(HALF + 1):
            both = [f] if f in (0, HALF) else [f, BLOCKS - f]
            rows = len(both) * ROWS // 2
            reals = [spec[g, :, :WIDE] for g in both]
            imags = [spec[g, :, WIDE:] for g in both]
            value = jnp.concatenate(reals + imags).astype(BF16)
            value = jnp.dot(value, weights[f], preferred_element_type=F32)
            real = value[:rows, :WIDE] - value[rows:, WIDE:]
            imag = value[:rows, WIDE:] + value[rows:, :WIDE]
            for i, g in enumerate(both):
                spec[g, :, :WIDE] = real[i * ROWS // 2 : (i + 1) * ROWS // 2]
                spec[g, :, WIDE:] = imag[i * ROWS // 2 : (i + 1) * ROWS // 2]

        pout[...] = jnp.zeros_like(pout)

        @pl.loop(0, PAIRS)
        def _(q):
            for f1 in range(8):
                points = []
                for f2 in range(8):
                    f = f1 + 8 * f2
                    real = spec[f, pl.ds(q * 8, 8), :WIDE]
                    imag = spec[f, pl.ds(q * 8, 8), WIDE:]
                    points.append((real, imag if f <= HALF else -imag))
                for n2, value in enumerate(swap(dft8(swap(points)))):
                    value = turn(value, -n2 * f1)
                    mid[n2 * 8 + f1, 0] = value[0]
                    mid[n2 * 8 + f1, 1] = value[1]
            for n2 in range(8):
                points = [(mid[n2 * 8 + f1, 0], mid[n2 * 8 + f1, 1]) for f1 in range(8)]
                for n1, value in enumerate(swap(dft8(swap(points)))):
                    n = 8 * n1 + n2
                    both = tile(c, q, n)
                    pout[n] += value[0] * both[:8] + value[1] * both[8:]
            pass

        @pl.loop(0, BLOCKS // 2)
        def _(i):
            zk, row = i // 8 * 2 + i % 2, i // 2 % 4
            for w in range(2):
                whole = pout[2 * i + w]
                whole = whole + pltpu.roll(whole, 4, 0)
                if c < MIXED:
                    for s in range(XS):
                        rs_snd[c, s, zk, row, w : w + 1] = whole[s : s + 1]
                else:
                    whole = whole + pltpu.roll(whole, 2, 0)
                    whole = whole + pltpu.roll(whole, 1, 0)
                    qb[c - MIXED + 1][zk, 0, row, w : w + 1] = whole[:1]

    def send_sums(c):
        for d in range(1, XS):
            remote(rs_snd.at[c, xs[d]], rs_rcv.at[c, d - 1], rs_send.at[c], rs_recv.at[c], lon, mems[d])

    def send_back(g):
        for j, c in enumerate(SETS[g]):
            if c < MIXED:
                done(rs_rcv.at[c], rs_recv.at[c])
                qb[g][:, j] = rs_snd[c, x] + rs_rcv[c, 0] + rs_rcv[c, 1] + rs_rcv[c, 2]
        mine = z * 2 + k
        for e in (1, 0):
            for s in range(8):
                if e or s:
                    index = zs[s // 2] // 4 + ks[s % 2]
                    remote(
                        qb[g].at[index], fr[g].at[zhi, mine], ret_send.at[g], ret_recv.at[g],
                        rows16[s], groups[e],
                    )
        local(qb[g].at[mine], fr[g].at[zhi, mine], ret_recv.at[g])

    def send_all(g):
        done(fr[g], ret_recv.at[g])
        for j in range(len(SETS[g])):
            for row in range(4):
                part[g][row, j] = fr[g][0, :, j, row] + fr[g][1, :, j, row]
        for d in (2, 1, 3, 0):
            for e in (2, 1, 3, 0):
                if d or e:
                    there = z * 8 + ys[e] + k
                    remote(
                        part[g].at[ys[e] // 2], fin[g].at[x, y], fin_send.at[g], fin_recv.at[g],
                        there, mems[d],
                    )
        local(part[g].at[y], fin[g].at[x, y], fin_recv.at[g])

    def assemble(g):
        done(fin[g], fin_recv.at[g])

        @pl.loop(0, 4)
        def _(row):
            for j, c in enumerate(SETS[g]):
                for s in range(XS):
                    for i in range(8):
                        to, at = i // 2 * 8 + row * 2 + i % 2, c * PER + s
                        out[to, at : at + 1, :WIDE] = fin[g][s, row, j, i, 0:1]
                        out[to, at : at + 1, WIDE:] = fin[g][s, row, j, i, 1:2]

    for step in range(CHUNKS):
        done(rcv.at[step], main_recv.at[step])
        if step == 0:
            pl.semaphore_wait(group_sem, 1)
        if step < 2:
            send_main(step + 1, 1)
        convolve(step)
        if step < MIXED:
            send_sums(step)
        else:
            send_back(step - 1)
        if step < 2:
            rearrange_mixed(step + 2)
            send_main(step + 2, 0)
        if step == 2:
            send_main(3, 1)
            send_back(0)
            send_all(1)

    send_all(0)
    assemble(1)
    send_all(2)
    assemble(0)
    assemble(2)

    @pl.when(lon % XS == x)
    def _():
        done(inc_in.at[pl.ds(0, (LONS - 1) * LATS)], inc_send)

    done(incb.at[three], incx_send)
    for c in range(CHUNKS):
        done(snd.at[c, pl.ds(0, LONS - 1)], main_send.at[c])
        if c >= MIXED:
            done(xsnd.at[c - MIXED, three], x_send.at[c - MIXED])
        if c < MIXED:
            done(rs_rcv.at[c], rs_send.at[c])
    for g in range(len(SETS)):
        done(fr[g].at[0], ret_send.at[g])
        done(fr[g].at[0, pl.ds(0, 7)], ret_send.at[g])
        done(fin[g].at[three], fin_send.at[g])
        done(fin[g].at[0, three], fin_send.at[g])


def per_device(anomalies, increment, spectral_taper):
    hbm, vmem = pl.BlockSpec(memory_space=pltpu.HBM), pl.BlockSpec(memory_space=pltpu.VMEM)
    constants = tables()
    dma = pltpu.SemaphoreType.DMA
    circle = (8, 4, 2, WIDE)
    mixed = (max(CHUNKS - MIXED, 1), XS, LONS // 2, 2 * MEMBERS, 2 * WIDE)
    total = pl.pallas_call(
        kernel,
        out_shape=jax.ShapeDtypeStruct((LONS, LATS, 2 * WIDE), F32),
        in_specs=[hbm] * 7,
        out_specs=vmem,
        scratch_shapes=[
            pltpu.VMEM((MEMBERS, LONS * LATS, 2 * WIDE), BF16),
            pltpu.VMEM((LONS * LATS, 2 * WIDE), BF16),
            pltpu.VMEM((BLOCKS, WIDE), F32),
        ]
        + [pltpu.VMEM(t.shape, F32) for t in constants]
        + [
            pltpu.VMEM((CHUNKS, LONS, ROWS, 2 * WIDE), BF16),
            pltpu.VMEM((CHUNKS, LONS, ROWS, 2 * WIDE), BF16),
            pltpu.VMEM(mixed, BF16),
            pltpu.VMEM(mixed, BF16),
            pltpu.VMEM((XS, LONS // XS, LATS, 2 * WIDE), BF16),
            pltpu.VMEM((CHUNKS, BLOCKS, 8, WIDE), F32),
            pltpu.VMEM((2, 40, 2 * WIDE), F32),
            pltpu.VMEM((HALF + 1, WIDE, 2 * WIDE), BF16),
            pltpu.VMEM((BLOCKS, ROWS // 2, 2 * WIDE), F32),
            pltpu.VMEM((BLOCKS, 2, 8, WIDE), F32),
            pltpu.VMEM((BLOCKS, 8, WIDE), F32),
            pltpu.VMEM((CHUNKS, XS) + circle, F32),
            pltpu.VMEM((CHUNKS, XS - 1) + circle, F32),
            dma((8,)), dma, dma, dma, dma, dma((CHUNKS,)), dma((CHUNKS,)),
            dma((CHUNKS,)), dma((CHUNKS,)), dma((CHUNKS,)), dma((CHUNKS,)), dma((CHUNKS,)), dma((CHUNKS,)),
            dma((CHUNKS,)), dma((CHUNKS,)), pltpu.SemaphoreType.REGULAR,
        ]
        + [pltpu.VMEM((8, len(g), 4, 2, WIDE), F32) for g in SETS]
        + [pltpu.VMEM((2, 8, len(g), 4, 2, WIDE), F32) for g in SETS]
        + [pltpu.VMEM((4, len(g), 8, 2, WIDE), F32) for g in SETS]
        + [pltpu.VMEM((XS, 4, len(g), 8, 2, WIDE), F32) for g in SETS],
        compiler_params=pltpu.CompilerParams(
            collective_id=0, has_side_effects=True, vmem_limit_bytes=62 << 20
        ),
        name="localize",
    )(anomalies, increment, spectral_taper.reshape(BLOCKS, WIDE), *constants)
    members = lax.axis_size("mem") * MEMBERS
    return total.reshape(LONS * LATS, 2 * WIDE) / (members - 1)


def solution(mesh):
    in_specs = (P("mem", None, "lon"), P(None, "lon"), P())
    return jax.shard_map(
        per_device, mesh=mesh, in_specs=in_specs, out_specs=P(None, "lon"), check_vma=False
    )
```

```python
import functools
import math

import jax
import jax.numpy as jnp
import numpy as np
from jax import lax
from jax.experimental import pallas as pl
from jax.experimental.pallas import tpu as pltpu
from jax.sharding import PartitionSpec as P

MESH = pl.DeviceIdType.MESH
NLON = 8192
BLOCKS = 64
WIDE = 128
HALF = BLOCKS // 2
LONS = 32
XS = 4
LATS = 16
CHUNKS = 4
SETS = ((0, 1), (2,), (3,))
MIXED = 2
PER = LATS // CHUNKS
MEMBERS = 8
ROWS = PER * MEMBERS
PAIRS = ROWS // 16
F32 = jnp.float32
BF16 = jnp.bfloat16


def tables():
    s = np.arange(WIDE)[:, None]
    r = np.arange(BLOCKS)[None, :]
    first = 2 * math.pi * (s * r % BLOCKS) / BLOCKS
    first = np.concatenate([np.cos(first), np.sin(first)], 0)
    c = np.arange(WIDE)[None, :]
    twist = 2 * math.pi * (s * c % NLON) / NLON
    twist = np.stack([np.cos(twist), np.sin(twist)])
    d = np.arange(BLOCKS)[:, None]
    back = 2 * math.pi * (d * c % BLOCKS) / BLOCKS
    back = np.stack([np.cos(back), np.sin(back)]) / (NLON * BLOCKS)
    f = np.arange(40)[:, None]
    d = np.arange(BLOCKS)[None, :]
    here = 2 * math.pi * (f * d % BLOCKS) / BLOCKS
    there = 2 * math.pi * (f * (d + 1) % BLOCKS) / BLOCKS
    again = np.stack([np.cos(here), -np.sin(here), np.cos(there), -np.sin(there)])
    return [np.asarray(t, np.float32) for t in (first, twist, back, again)]


def dft4(x):
    (ar, ai), (br, bi), (cr, ci), (dr, di) = x
    er, ei, fr, fi = ar + cr, ai + ci, ar - cr, ai - ci
    gr, gi, hr, hi = br + dr, bi + di, br - dr, bi - di
    return [(er + gr, ei + gi), (fr + hi, fi - hr), (er - gr, ei - gi), (fr - hi, fi + hr)]


def dft8(x):
    even, odd = dft4(x[0::2]), dft4(x[1::2])
    root = math.sqrt(0.5)
    (ar, ai), (br, bi), (cr, ci), (dr, di) = odd
    turned = [
        (ar, ai),
        ((br + bi) * root, (bi - br) * root),
        (ci, -cr),
        ((di - dr) * root, (dr + di) * -root),
    ]
    low = [(e[0] + t[0], e[1] + t[1]) for e, t in zip(even, turned)]
    high = [(e[0] - t[0], e[1] - t[1]) for e, t in zip(even, turned)]
    return low + high


def swap(x):
    return [(i, r) for r, i in x]


def turn(x, power):
    power = power % BLOCKS
    if power == 0:
        return x
    c = math.cos(2 * math.pi * power / BLOCKS)
    s = -math.sin(2 * math.pi * power / BLOCKS)
    return (x[0] * c - x[1] * s, x[0] * s + x[1] * c)


def high(a, b, dims=((1,), (0,))):
    return lax.dot_general(
        a, b, (dims, ((), ())), precision=lax.Precision.HIGHEST, preferred_element_type=F32
    )


def kernel(
    a_hbm, inc_hbm, taper_hbm, first_hbm, twist_hbm, back_hbm, again_hbm, out,
    a_in, inc_in, taper, first, twist, back, again,
    snd, rcv, xsnd, xrcv, incb, incf, lines, weights, spec, mid, pout, rs_snd, rs_rcv,
    load_sem, inc_send, inc_recv, incx_send, incx_recv, main_send, main_recv,
    x_send, x_recv, rs_send, rs_recv, ret_send, ret_recv, fin_send, fin_recv, group_sem, *sums,
):
    lon, mem = lax.axis_index("lon"), lax.axis_index("mem")
    z, y, k = lon // 8, (lon // 2) % 4, lon % 2
    zhi, x = mem // XS, mem % XS

    qb, fr, part, fin = [sums[i * len(SETS) : (i + 1) * len(SETS)] for i in range(4)]

    def load(source, target, sem):
        copy = pltpu.make_async_copy(source, target, load_sem.at[sem])
        copy.start()
        return copy

    group = MEMBERS // 2
    load_a = [load(a_hbm.at[pl.ds(j * group, group)], a_in.at[pl.ds(j * group, group)], j) for j in range(2)]

    def after(v, d):
        return (v + d) % 4

    zs = [after(z, d) * 8 for d in range(4)]
    ys = [after(y, d) * 2 for d in range(4)]
    ks = [k, 1 - k]
    peers = [zs[s // 8] + ys[s // 2 % 4] + ks[s % 2] for s in range(LONS)]
    xs = [(x + d) % XS for d in range(XS)]
    mems = [zhi * XS + xs[d] for d in range(XS)]
    groups = [mem, (1 - zhi) * XS + x]
    rows16 = [zs[s // 2] + ys[0] + ks[s % 2] for s in range(8)]

    barrier = pltpu.get_barrier_semaphore()

    def greet(there, group):
        pl.semaphore_signal(
            barrier, inc=1, device_id={"lon": there, "mem": group}, device_id_type=MESH
        )

    greet(lon, groups[1])
    for s in reversed(range(1, LONS)):
        greet(peers[s], mem)
    for d in range(1, XS):
        greet(lon, mems[d])

    load_i = load(inc_hbm, inc_in, 2)
    pairs = [(taper_hbm, taper), (first_hbm, first), (twist_hbm, twist), (back_hbm, back), (again_hbm, again)]
    load_t = [load(a, b, 3 + i) for i, (a, b) in enumerate(pairs)]

    def remote(source, target, send, recv, there, group):
        pltpu.make_async_remote_copy(
            src_ref=source, dst_ref=target, send_sem=send, recv_sem=recv,
            device_id={"lon": there, "mem": group}, device_id_type=MESH,
        ).start()

    def local(source, target, sem):
        pltpu.make_async_copy(source, target, sem).start()

    def done(ref, sem):
        pltpu.make_async_copy(ref, ref, sem).wait()

    wanted = lax.broadcasted_iota(jnp.int32, (8, WIDE), 0)
    upper = wanted < PER

    def rearrange(c):
        half, low = c // 2, c % 2 == 0

        @pl.loop(0, LONS)
        def _(t):
            for w in range(2):
                cols = slice(w * WIDE, (w + 1) * WIDE)
                parts = []
                for j in range(MEMBERS):
                    whole = a_in[j, pl.ds(t * LATS, LATS), cols].astype(F32)
                    parts.append(whole[half * 8 : half * 8 + 8])
                for j in range(0, MEMBERS, 4):
                    rows = []
                    for i in (j, j + 2):
                        one, two = parts[i], parts[i + 1]
                        if low:
                            two = pltpu.roll(two, PER, 0)
                        else:
                            one = pltpu.roll(one, PER, 0)
                        rows.append(jnp.where(upper, one, two))
                    snd[c, t, pl.ds(j * PER, 4 * PER), cols] = jnp.concatenate(rows).astype(BF16)

    def gather_x():
        row = lax.broadcasted_iota(jnp.int32, (XS * MEMBERS, MEMBERS * LATS), 0)
        col = lax.broadcasted_iota(jnp.int32, (XS * MEMBERS, MEMBERS * LATS), 1)
        for c in range(MIXED, CHUNKS):
            pick = (col == row % MEMBERS * LATS + c * PER + row // MEMBERS).astype(BF16)

            @pl.loop(0, LONS // 2)
            def _(u):
                picked = []
                for e in range(2):
                    whole = a_in[:, pl.ds((2 * u + e) * LATS, LATS), :]
                    whole = whole.reshape(MEMBERS * LATS, 2 * WIDE)
                    picked.append(jnp.dot(pick, whole, preferred_element_type=F32))
                for s in range(XS):
                    both = [p[s * MEMBERS : (s + 1) * MEMBERS] for p in picked]
                    xsnd[c - MIXED, s, u] = jnp.concatenate(both).astype(BF16)

    def send_x(c):
        m = c - MIXED
        for d in range(1, XS):
            remote(xsnd.at[m, xs[d]], xrcv.at[m, x], x_send.at[m], x_recv.at[m], lon, mems[d])
        local(xsnd.at[m, x], xrcv.at[m, x], x_recv.at[m])

    def rearrange_mixed(c):
        m = c - MIXED
        done(xrcv.at[m], x_recv.at[m])

        @pl.loop(0, LONS // 2)
        def _(u):
            for s in range(0, XS, 2):
                one, two = xrcv[m, s, u].astype(F32), xrcv[m, s + 1, u].astype(F32)
                for e in range(2):
                    both = [v[e * MEMBERS : (e + 1) * MEMBERS] for v in (one, two)]
                    snd[c, 2 * u + e, s * MEMBERS : (s + 2) * MEMBERS] = jnp.concatenate(both).astype(BF16)

    def send_main(c, half):
        if c == CHUNKS - 1:
            rows, sem = pl.ds(half * 16, 16), main_recv.at[c + half]
            for s in range(1, LONS):
                remote(snd.at[c, peers[s], rows], rcv.at[c, lon, rows], main_send.at[c], sem, peers[s], mem)
            local(snd.at[c, lon, rows], rcv.at[c, lon, rows], sem)
            return
        for s in range(1, LONS):
            if s % 2 == half:
                remote(snd.at[c, peers[s]], rcv.at[c, lon], main_send.at[c], main_recv.at[c], peers[s], mem)
        if half:
            local(snd.at[c, lon], rcv.at[c, lon], main_recv.at[c])

    for copy in load_a:
        copy.wait()
    rearrange(0)
    load_i.wait()
    pl.semaphore_wait(barrier, LONS + XS - 1)
    pl.semaphore_signal(
        group_sem, inc=1, device_id={"lon": lon, "mem": groups[1]}, device_id_type=MESH
    )

    send_main(0, 0)
    pl.semaphore_wait(group_sem, 1)

    @pl.when(lon % XS == x)
    def _():
        for s in range(1, LONS):
            block = inc_in.at[pl.ds(peers[s] * LATS, LATS)]
            beyond = (z // 2 + peers[s] // 16) % 2
            there = (zhi + beyond) % 2 * XS + x
            remote(block, incb.at[x, lon // XS], inc_send, inc_recv, peers[s], there)
        local(inc_in.at[pl.ds(lon * LATS, LATS)], incb.at[x, lon // XS], inc_recv)

    send_main(0, 1)
    for c in range(1, MIXED):
        rearrange(c)
    gather_x()
    done(incb.at[x], inc_recv)
    for d in range(1, XS):
        remote(incb.at[x], incb.at[x], incx_send, incx_recv, lon, mems[d])
    for c in range(MIXED, CHUNKS):
        send_x(c)
    send_main(1, 0)

    for copy in load_t:
        copy.wait()

    u = high(first[...], taper[...])
    ur, ui = u[:WIDE], u[WIDE:]
    vr = ur * twist[0] - ui * twist[1]
    vi = ur * twist[1] + ui * twist[0]
    line = high(back[0], vr, ((1,), (1,))) - high(back[1], vi, ((1,), (1,)))
    lines[0, :, :WIDE] = high(again[0], line)
    lines[1, :, :WIDE] = high(again[1], line)
    lines[0, :, WIDE:] = high(again[2], line)
    lines[1, :, WIDE:] = high(again[3], line)

    @pl.loop(0, HALF + 1)
    def _(f):
        def toeplitz(part):
            row = jnp.broadcast_to(lines[part, pl.ds(f, 1), :], (WIDE, 2 * WIDE))
            return pltpu.roll(row, 0, 1, stride=1, stride_axis=0)[:, :WIDE]

        real, imag = toeplitz(0), toeplitz(1)
        weights[f, :, :WIDE] = real.astype(BF16)
        weights[f, :, WIDE:] = imag.astype(BF16)

    three = pl.ds(0, XS - 1)
    done(incb.at[three], incx_recv)

    @pl.loop(0, LONS)
    def _(i):
        for w in range(2):
            whole = incb[i % XS, i // XS, :, w * WIDE : (w + 1) * WIDE].astype(F32)
            for c in range(CHUNKS):
                part = whole[c // 2 * 8 : c // 2 * 8 + 8]
                turned = pltpu.roll(part, PER, 0)
                one, two = (part, turned) if c % 2 == 0 else (turned, part)
                if c < MIXED:
                    incf[c, 2 * i + w] = jnp.where(upper, one, two)
                else:
                    mine = jnp.where(wanted == c % 2 * PER + x, part, 0.0)
                    mine = jnp.sum(mine, axis=0, keepdims=True)
                    incf[c, 2 * i + w] = jnp.broadcast_to(mine, (8, WIDE))

    def tile(c, q, n):
        return rcv[c, n // 2, pl.ds(q * 16, 16), (n % 2) * WIDE : (n % 2 + 1) * WIDE].astype(F32)

    def convolve(c, qs):
        top, count = qs[0] * 8, len(qs) * 8
        @pl.loop(qs[0], qs[-1] + 1)
        def _(q):
            for n2 in range(8):
                points = []
                for n1 in range(8):
                    n = 8 * n1 + n2
                    both = tile(c, q, n)
                    field = incf[c, n]
                    real = (both[:8] * field).astype(BF16).astype(F32)
                    imag = (both[8:] * field).astype(BF16).astype(F32)
                    points.append((real, imag))
                for f1, value in enumerate(dft8(points)):
                    value = turn(value, n2 * f1)
                    mid[f1 * 8 + n2, 0] = value[0]
                    mid[f1 * 8 + n2, 1] = value[1]
            for f1 in range(8):
                points = [(mid[f1 * 8 + n2, 0], mid[f1 * 8 + n2, 1]) for n2 in range(8)]
                for f2, value in enumerate(dft8(points)):
                    f = f1 + 8 * f2
                    spec[f, pl.ds(q * 8, 8), :WIDE] = value[0]
                    spec[f, pl.ds(q * 8, 8), WIDE:] = value[1] if f <= HALF else -value[1]
            pass

        for f in range(HALF + 1):
            both = [f] if f in (0, HALF) else [f, BLOCKS - f]
            rows = len(both) * count
            reals = [spec[g, top : top + count, :WIDE] for g in both]
            imags = [spec[g, top : top + count, WIDE:] for g in both]
            value = jnp.concatenate(reals + imags).astype(BF16)
            value = jnp.dot(value, weights[f], preferred_element_type=F32)
            real = value[:rows, :WIDE] - value[rows:, WIDE:]
            imag = value[:rows, WIDE:] + value[rows:, :WIDE]
            for i, g in enumerate(both):
                spec[g, top : top + count, :WIDE] = real[i * count : (i + 1) * count]
                spec[g, top : top + count, WIDE:] = imag[i * count : (i + 1) * count]

        if top == 0:
            pout[...] = jnp.zeros_like(pout)

        @pl.loop(qs[0], qs[-1] + 1)
        def _(q):
            for f1 in range(8):
                points = []
                for f2 in range(8):
                    f = f1 + 8 * f2
                    real = spec[f, pl.ds(q * 8, 8), :WIDE]
                    imag = spec[f, pl.ds(q * 8, 8), WIDE:]
                    points.append((real, imag if f <= HALF else -imag))
                for n2, value in enumerate(swap(dft8(swap(points)))):
                    value = turn(value, -n2 * f1)
                    mid[n2 * 8 + f1, 0] = value[0]
                    mid[n2 * 8 + f1, 1] = value[1]
            for n2 in range(8):
                points = [(mid[n2 * 8 + f1, 0], mid[n2 * 8 + f1, 1]) for f1 in range(8)]
                for n1, value in enumerate(swap(dft8(swap(points)))):
                    n = 8 * n1 + n2
                    both = tile(c, q, n)
                    pout[n] += value[0] * both[:8] + value[1] * both[8:]
            pass

        if qs[-1] + 1 < PAIRS:
            return

        @pl.loop(0, BLOCKS // 2)
        def _(i):
            zk, row = i // 8 * 2 + i % 2, i // 2 % 4
            for w in range(2):
                whole = pout[2 * i + w]
                whole = whole + pltpu.roll(whole, 4, 0)
                if c < MIXED:
                    for s in range(XS):
                        rs_snd[c, s, zk, row, w : w + 1] = whole[s : s + 1]
                else:
                    whole = whole + pltpu.roll(whole, 2, 0)
                    whole = whole + pltpu.roll(whole, 1, 0)
                    qb[c - MIXED + 1][zk, 0, row, w : w + 1] = whole[:1]

    def send_sums(c):
        for d in range(1, XS):
            remote(rs_snd.at[c, xs[d]], rs_rcv.at[c, d - 1], rs_send.at[c], rs_recv.at[c], lon, mems[d])

    def send_back(g):
        for j, c in enumerate(SETS[g]):
            if c < MIXED:
                done(rs_rcv.at[c], rs_recv.at[c])
                qb[g][:, j] = rs_snd[c, x] + rs_rcv[c, 0] + rs_rcv[c, 1] + rs_rcv[c, 2]
        mine = z * 2 + k
        for e in (1, 0):
            for s in range(8):
                if e or s:
                    index = zs[s // 2] // 4 + ks[s % 2]
                    remote(
                        qb[g].at[index], fr[g].at[zhi, mine], ret_send.at[g], ret_recv.at[g],
                        rows16[s], groups[e],
                    )
        local(qb[g].at[mine], fr[g].at[zhi, mine], ret_recv.at[g])

    def send_all(g):
        done(fr[g], ret_recv.at[g])
        for j in range(len(SETS[g])):
            for row in range(4):
                part[g][row, j] = fr[g][0, :, j, row] + fr[g][1, :, j, row]
        for d in (2, 1, 3, 0):
            for e in (2, 1, 3, 0):
                if d or e:
                    there = z * 8 + ys[e] + k
                    remote(
                        part[g].at[ys[e] // 2], fin[g].at[x, y], fin_send.at[g], fin_recv.at[g],
                        there, mems[d],
                    )
        local(part[g].at[y], fin[g].at[x, y], fin_recv.at[g])

    def assemble(g):
        done(fin[g], fin_recv.at[g])

        @pl.loop(0, 4)
        def _(row):
            for j, c in enumerate(SETS[g]):
                for s in range(XS):
                    for i in range(8):
                        to, at = i // 2 * 8 + row * 2 + i % 2, c * PER + s
                        out[to, at : at + 1, :WIDE] = fin[g][s, row, j, i, 0:1]
                        out[to, at : at + 1, WIDE:] = fin[g][s, row, j, i, 1:2]

    for step in range(CHUNKS):
        if step < CHUNKS - 1:
            done(rcv.at[step], main_recv.at[step])
        if step < 2:
            send_main(step + 1, 1)
        if step < CHUNKS - 1:
            convolve(step, range(PAIRS))
        else:
            for q in range(PAIRS):
                done(rcv.at[step, pl.ds(0, LONS), pl.ds(q * 16, 16)], main_recv.at[step + q])
                convolve(step, (q,))
        if step < MIXED:
            send_sums(step)
        else:
            send_back(step - 1)
        if step < 2:
            rearrange_mixed(step + 2)
            send_main(step + 2, 0)
        if step == 2:
            send_main(3, 1)
            send_back(0)
            send_all(1)

    send_all(0)
    assemble(1)
    send_all(2)
    assemble(0)
    assemble(2)

    @pl.when(lon % XS == x)
    def _():
        done(inc_in.at[pl.ds(0, (LONS - 1) * LATS)], inc_send)

    done(incb.at[three], incx_send)
    for c in range(CHUNKS):
        done(snd.at[c, pl.ds(0, LONS - 1)], main_send.at[c])
        if c >= MIXED:
            done(xsnd.at[c - MIXED, three], x_send.at[c - MIXED])
        if c < MIXED:
            done(rs_rcv.at[c], rs_send.at[c])
    for g in range(len(SETS)):
        done(fr[g].at[0], ret_send.at[g])
        done(fr[g].at[0, pl.ds(0, 7)], ret_send.at[g])
        done(fin[g].at[three], fin_send.at[g])
        done(fin[g].at[0, three], fin_send.at[g])


def per_device(anomalies, increment, spectral_taper):
    hbm, vmem = pl.BlockSpec(memory_space=pltpu.HBM), pl.BlockSpec(memory_space=pltpu.VMEM)
    constants = tables()
    dma = pltpu.SemaphoreType.DMA
    circle = (8, 4, 2, WIDE)
    mixed = (max(CHUNKS - MIXED, 1), XS, LONS // 2, 2 * MEMBERS, 2 * WIDE)
    total = pl.pallas_call(
        kernel,
        out_shape=jax.ShapeDtypeStruct((LONS, LATS, 2 * WIDE), F32),
        in_specs=[hbm] * 7,
        out_specs=vmem,
        scratch_shapes=[
            pltpu.VMEM((MEMBERS, LONS * LATS, 2 * WIDE), BF16),
            pltpu.VMEM((LONS * LATS, 2 * WIDE), BF16),
            pltpu.VMEM((BLOCKS, WIDE), F32),
        ]
        + [pltpu.VMEM(t.shape, F32) for t in constants]
        + [
            pltpu.VMEM((CHUNKS, LONS, ROWS, 2 * WIDE), BF16),
            pltpu.VMEM((CHUNKS, LONS, ROWS, 2 * WIDE), BF16),
            pltpu.VMEM(mixed, BF16),
            pltpu.VMEM(mixed, BF16),
            pltpu.VMEM((XS, LONS // XS, LATS, 2 * WIDE), BF16),
            pltpu.VMEM((CHUNKS, BLOCKS, 8, WIDE), F32),
            pltpu.VMEM((2, 40, 2 * WIDE), F32),
            pltpu.VMEM((HALF + 1, WIDE, 2 * WIDE), BF16),
            pltpu.VMEM((BLOCKS, ROWS // 2, 2 * WIDE), F32),
            pltpu.VMEM((BLOCKS, 2, 8, WIDE), F32),
            pltpu.VMEM((BLOCKS, 8, WIDE), F32),
            pltpu.VMEM((CHUNKS, XS) + circle, F32),
            pltpu.VMEM((CHUNKS, XS - 1) + circle, F32),
            dma((8,)), dma, dma, dma, dma, dma((CHUNKS,)), dma((CHUNKS + 1,)),
            dma((CHUNKS,)), dma((CHUNKS,)), dma((CHUNKS,)), dma((CHUNKS,)), dma((CHUNKS,)), dma((CHUNKS,)),
            dma((CHUNKS,)), dma((CHUNKS,)), pltpu.SemaphoreType.REGULAR,
        ]
        + [pltpu.VMEM((8, len(g), 4, 2, WIDE), F32) for g in SETS]
        + [pltpu.VMEM((2, 8, len(g), 4, 2, WIDE), F32) for g in SETS]
        + [pltpu.VMEM((4, len(g), 8, 2, WIDE), F32) for g in SETS]
        + [pltpu.VMEM((XS, 4, len(g), 8, 2, WIDE), F32) for g in SETS],
        compiler_params=pltpu.CompilerParams(
            collective_id=0, has_side_effects=True, vmem_limit_bytes=62 << 20
        ),
        name="localize",
    )(anomalies, increment, spectral_taper.reshape(BLOCKS, WIDE), *constants)
    members = lax.axis_size("mem") * MEMBERS
    return total.reshape(LONS * LATS, 2 * WIDE) / (members - 1)


def solution(mesh):
    in_specs = (P("mem", None, "lon"), P(None, "lon"), P())
    return jax.shard_map(
        per_device, mesh=mesh, in_specs=in_specs, out_specs=P(None, "lon"), check_vma=False
    )
```

```python
import functools
import math

import jax
import jax.numpy as jnp
import numpy as np
from jax import lax
from jax.experimental import pallas as pl
from jax.experimental.pallas import tpu as pltpu
from jax.sharding import PartitionSpec as P

MESH = pl.DeviceIdType.MESH
NLON = 8192
BLOCKS = 64
WIDE = 128
HALF = BLOCKS // 2
LONS = 32
XS = 4
LATS = 16
CHUNKS = 4
SETS = ((0, 1), (2,), (3,))
MIXED = 2
PER = LATS // CHUNKS
MEMBERS = 8
ROWS = PER * MEMBERS
PAIRS = ROWS // 16
F32 = jnp.float32
BF16 = jnp.bfloat16


def tables():
    s = np.arange(WIDE)[:, None]
    r = np.arange(BLOCKS)[None, :]
    first = 2 * math.pi * (s * r % BLOCKS) / BLOCKS
    first = np.concatenate([np.cos(first), np.sin(first)], 0)
    c = np.arange(WIDE)[None, :]
    twist = 2 * math.pi * (s * c % NLON) / NLON
    twist = np.stack([np.cos(twist), np.sin(twist)])
    d = np.arange(BLOCKS)[:, None]
    back = 2 * math.pi * (d * c % BLOCKS) / BLOCKS
    back = np.stack([np.cos(back), np.sin(back)]) / (NLON * BLOCKS)
    f = np.arange(40)[:, None]
    d = np.arange(BLOCKS)[None, :]
    here = 2 * math.pi * (f * d % BLOCKS) / BLOCKS
    there = 2 * math.pi * (f * (d + 1) % BLOCKS) / BLOCKS
    again = np.stack([np.cos(here), -np.sin(here), np.cos(there), -np.sin(there)])
    return [np.asarray(t, np.float32) for t in (first, twist, back, again)]


def dft4(x):
    (ar, ai), (br, bi), (cr, ci), (dr, di) = x
    er, ei, fr, fi = ar + cr, ai + ci, ar - cr, ai - ci
    gr, gi, hr, hi = br + dr, bi + di, br - dr, bi - di
    return [(er + gr, ei + gi), (fr + hi, fi - hr), (er - gr, ei - gi), (fr - hi, fi + hr)]


def dft8(x):
    even, odd = dft4(x[0::2]), dft4(x[1::2])
    root = math.sqrt(0.5)
    (ar, ai), (br, bi), (cr, ci), (dr, di) = odd
    turned = [
        (ar, ai),
        ((br + bi) * root, (bi - br) * root),
        (ci, -cr),
        ((di - dr) * root, (dr + di) * -root),
    ]
    low = [(e[0] + t[0], e[1] + t[1]) for e, t in zip(even, turned)]
    high = [(e[0] - t[0], e[1] - t[1]) for e, t in zip(even, turned)]
    return low + high


def swap(x):
    return [(i, r) for r, i in x]


def turn(x, power):
    power = power % BLOCKS
    if power == 0:
        return x
    c = math.cos(2 * math.pi * power / BLOCKS)
    s = -math.sin(2 * math.pi * power / BLOCKS)
    return (x[0] * c - x[1] * s, x[0] * s + x[1] * c)


def high(a, b, dims=((1,), (0,))):
    return lax.dot_general(
        a, b, (dims, ((), ())), precision=lax.Precision.HIGHEST, preferred_element_type=F32
    )


def kernel(
    a_hbm, inc_hbm, taper_hbm, first_hbm, twist_hbm, back_hbm, again_hbm, out,
    a_in, inc_in, taper, first, twist, back, again,
    snd, rcv, xsnd, xrcv, incb, incf, lines, weights, spec, mid, pout, rs_snd, rs_rcv,
    load_sem, inc_send, inc_recv, incx_send, incx_recv, main_send, main_recv,
    x_send, x_recv, rs_send, rs_recv, ret_send, ret_recv, fin_send, fin_recv, group_sem, *sums,
):
    lon, mem = lax.axis_index("lon"), lax.axis_index("mem")
    z, y, k = lon // 8, (lon // 2) % 4, lon % 2
    zhi, x = mem // XS, mem % XS

    qb, fr, part, fin = [sums[i * len(SETS) : (i + 1) * len(SETS)] for i in range(4)]

    def load(source, target, sem):
        copy = pltpu.make_async_copy(source, target, load_sem.at[sem])
        copy.start()
        return copy

    group = MEMBERS // 2
    load_a = [load(a_hbm.at[pl.ds(j * group, group)], a_in.at[pl.ds(j * group, group)], j) for j in range(2)]

    def after(v, d):
        return (v + d) % 4

    zs = [after(z, d) * 8 for d in range(4)]
    ys = [after(y, d) * 2 for d in range(4)]
    ks = [k, 1 - k]
    peers = [zs[s // 8] + ys[s // 2 % 4] + ks[s % 2] for s in range(LONS)]
    xs = [(x + d) % XS for d in range(XS)]
    mems = [zhi * XS + xs[d] for d in range(XS)]
    groups = [mem, (1 - zhi) * XS + x]
    rows16 = [zs[s // 2] + ys[0] + ks[s % 2] for s in range(8)]

    barrier = pltpu.get_barrier_semaphore()

    def greet(there, group):
        pl.semaphore_signal(
            barrier, inc=1, device_id={"lon": there, "mem": group}, device_id_type=MESH
        )

    greet(lon, groups[1])
    for s in reversed(range(1, LONS)):
        greet(peers[s], mem)
    for d in range(1, XS):
        greet(lon, mems[d])

    load_i = load(inc_hbm, inc_in, 2)
    pairs = [(taper_hbm, taper), (first_hbm, first), (twist_hbm, twist), (back_hbm, back), (again_hbm, again)]
    load_t = [load(a, b, 3 + i) for i, (a, b) in enumerate(pairs)]

    def remote(source, target, send, recv, there, group):
        pltpu.make_async_remote_copy(
            src_ref=source, dst_ref=target, send_sem=send, recv_sem=recv,
            device_id={"lon": there, "mem": group}, device_id_type=MESH,
        ).start()

    def local(source, target, sem):
        pltpu.make_async_copy(source, target, sem).start()

    def done(ref, sem):
        pltpu.make_async_copy(ref, ref, sem).wait()

    wanted = lax.broadcasted_iota(jnp.int32, (8, WIDE), 0)
    upper = wanted < PER

    def rearrange(c):
        half, low = c // 2, c % 2 == 0

        @pl.loop(0, LONS)
        def _(t):
            for w in range(2):
                cols = slice(w * WIDE, (w + 1) * WIDE)
                parts = []
                for j in range(MEMBERS):
                    whole = a_in[j, pl.ds(t * LATS, LATS), cols].astype(F32)
                    parts.append(whole[half * 8 : half * 8 + 8])
                for j in range(0, MEMBERS, 4):
                    rows = []
                    for i in (j, j + 2):
                        one, two = parts[i], parts[i + 1]
                        if low:
                            two = pltpu.roll(two, PER, 0)
                        else:
                            one = pltpu.roll(one, PER, 0)
                        rows.append(jnp.where(upper, one, two))
                    snd[c, t, pl.ds(j * PER, 4 * PER), cols] = jnp.concatenate(rows).astype(BF16)

    def gather_x():
        row = lax.broadcasted_iota(jnp.int32, (XS * MEMBERS, MEMBERS * LATS), 0)
        col = lax.broadcasted_iota(jnp.int32, (XS * MEMBERS, MEMBERS * LATS), 1)
        for c in range(MIXED, CHUNKS):
            pick = (col == row % MEMBERS * LATS + c * PER + row // MEMBERS).astype(BF16)

            @pl.loop(0, LONS // 2)
            def _(u):
                picked = []
                for e in range(2):
                    whole = a_in[:, pl.ds((2 * u + e) * LATS, LATS), :]
                    whole = whole.reshape(MEMBERS * LATS, 2 * WIDE)
                    picked.append(jnp.dot(pick, whole, preferred_element_type=F32))
                for s in range(XS):
                    both = [p[s * MEMBERS : (s + 1) * MEMBERS] for p in picked]
                    xsnd[c - MIXED, s, u] = jnp.concatenate(both).astype(BF16)

    def send_x(c):
        m = c - MIXED
        for d in range(1, XS):
            remote(xsnd.at[m, xs[d]], xrcv.at[m, x], x_send.at[m], x_recv.at[m], lon, mems[d])
        local(xsnd.at[m, x], xrcv.at[m, x], x_recv.at[m])

    def rearrange_mixed(c):
        m = c - MIXED
        done(xrcv.at[m], x_recv.at[m])

        @pl.loop(0, LONS // 2)
        def _(u):
            for s in range(0, XS, 2):
                one, two = xrcv[m, s, u].astype(F32), xrcv[m, s + 1, u].astype(F32)
                for e in range(2):
                    both = [v[e * MEMBERS : (e + 1) * MEMBERS] for v in (one, two)]
                    snd[c, 2 * u + e, s * MEMBERS : (s + 2) * MEMBERS] = jnp.concatenate(both).astype(BF16)

    def send_main(c, half):
        if c == CHUNKS - 1:
            rows, sem = pl.ds(half * 16, 16), main_recv.at[c + half]
            for s in range(1, LONS):
                remote(snd.at[c, peers[s], rows], rcv.at[c, lon, rows], main_send.at[c], sem, peers[s], mem)
            local(snd.at[c, lon, rows], rcv.at[c, lon, rows], sem)
            return
        for s in range(1, LONS):
            if s % 2 == half:
                remote(snd.at[c, peers[s]], rcv.at[c, lon], main_send.at[c], main_recv.at[c], peers[s], mem)
        if half:
            local(snd.at[c, lon], rcv.at[c, lon], main_recv.at[c])

    for copy in load_a:
        copy.wait()
    rearrange(0)
    load_i.wait()
    pl.semaphore_wait(barrier, LONS + XS - 1)
    pl.semaphore_signal(
        group_sem, inc=1, device_id={"lon": lon, "mem": groups[1]}, device_id_type=MESH
    )

    send_main(0, 0)
    pl.semaphore_wait(group_sem, 1)

    @pl.when(lon % XS == x)
    def _():
        for s in range(1, LONS):
            block = inc_in.at[pl.ds(peers[s] * LATS, LATS)]
            beyond = (z // 2 + peers[s] // 16) % 2
            there = (zhi + beyond) % 2 * XS + x
            remote(block, incb.at[x, lon // XS], inc_send, inc_recv, peers[s], there)
        local(inc_in.at[pl.ds(lon * LATS, LATS)], incb.at[x, lon // XS], inc_recv)

    send_main(0, 1)
    for c in range(1, MIXED):
        rearrange(c)
    gather_x()
    done(incb.at[x], inc_recv)
    for d in range(1, XS):
        remote(incb.at[x], incb.at[x], incx_send, incx_recv, lon, mems[d])
    for c in range(MIXED, CHUNKS):
        send_x(c)
    send_main(1, 0)

    for copy in load_t:
        copy.wait()

    u = high(first[...], taper[...])
    ur, ui = u[:WIDE], u[WIDE:]
    vr = ur * twist[0] - ui * twist[1]
    vi = ur * twist[1] + ui * twist[0]
    line = high(back[0], vr, ((1,), (1,))) - high(back[1], vi, ((1,), (1,)))
    lines[0, :, :WIDE] = high(again[0], line)
    lines[1, :, :WIDE] = high(again[1], line)
    lines[0, :, WIDE:] = high(again[2], line)
    lines[1, :, WIDE:] = high(again[3], line)

    @pl.loop(0, HALF + 1)
    def _(f):
        def toeplitz(part):
            row = jnp.broadcast_to(lines[part, pl.ds(f, 1), :], (WIDE, 2 * WIDE))
            return pltpu.roll(row, 0, 1, stride=1, stride_axis=0)[:, :WIDE]

        real, imag = toeplitz(0), toeplitz(1)
        weights[f, :, :WIDE] = real.astype(BF16)
        weights[f, :, WIDE:] = imag.astype(BF16)

    three = pl.ds(0, XS - 1)
    done(incb.at[three], incx_recv)

    @pl.loop(0, LONS)
    def _(i):
        for w in range(2):
            whole = incb[i % XS, i // XS, :, w * WIDE : (w + 1) * WIDE].astype(F32)
            for c in range(CHUNKS):
                part = whole[c // 2 * 8 : c // 2 * 8 + 8]
                turned = pltpu.roll(part, PER, 0)
                one, two = (part, turned) if c % 2 == 0 else (turned, part)
                if c < MIXED:
                    incf[c, 2 * i + w] = jnp.where(upper, one, two)
                else:
                    mine = jnp.where(wanted == c % 2 * PER + x, part, 0.0)
                    mine = jnp.sum(mine, axis=0, keepdims=True)
                    incf[c, 2 * i + w] = jnp.broadcast_to(mine, (8, WIDE))

    def tile(c, q, n):
        return rcv[c, n // 2, pl.ds(q * 16, 16), (n % 2) * WIDE : (n % 2 + 1) * WIDE].astype(F32)

    def convolve(c, qs):
        top, count = qs[0] * 8, len(qs) * 8
        @pl.loop(qs[0], qs[-1] + 1)
        def _(q):
            for n2 in range(8):
                points = []
                for n1 in range(8):
                    n = 8 * n1 + n2
                    both = tile(c, q, n)
                    field = incf[c, n]
                    real = (both[:8] * field).astype(BF16).astype(F32)
                    imag = (both[8:] * field).astype(BF16).astype(F32)
                    points.append((real, imag))
                for f1, value in enumerate(dft8(points)):
                    value = turn(value, n2 * f1)
                    mid[f1 * 8 + n2, 0] = value[0]
                    mid[f1 * 8 + n2, 1] = value[1]
            for f1 in range(8):
                points = [(mid[f1 * 8 + n2, 0], mid[f1 * 8 + n2, 1]) for n2 in range(8)]
                for f2, value in enumerate(dft8(points)):
                    f = f1 + 8 * f2
                    spec[f, pl.ds(q * 8, 8), :WIDE] = value[0]
                    spec[f, pl.ds(q * 8, 8), WIDE:] = value[1] if f <= HALF else -value[1]
            pass

        for f in range(HALF + 1):
            both = [f] if f in (0, HALF) else [f, BLOCKS - f]
            rows = len(both) * count
            reals = [spec[g, top : top + count, :WIDE] for g in both]
            imags = [spec[g, top : top + count, WIDE:] for g in both]
            value = jnp.concatenate(reals + imags).astype(BF16)
            value = jnp.dot(value, weights[f], preferred_element_type=F32)
            real = value[:rows, :WIDE] - value[rows:, WIDE:]
            imag = value[:rows, WIDE:] + value[rows:, :WIDE]
            for i, g in enumerate(both):
                spec[g, top : top + count, :WIDE] = real[i * count : (i + 1) * count]
                spec[g, top : top + count, WIDE:] = imag[i * count : (i + 1) * count]

        if top == 0:
            pout[...] = jnp.zeros_like(pout)

        @pl.loop(qs[0], qs[-1] + 1)
        def _(q):
            for f1 in range(8):
                points = []
                for f2 in range(8):
                    f = f1 + 8 * f2
                    real = spec[f, pl.ds(q * 8, 8), :WIDE]
                    imag = spec[f, pl.ds(q * 8, 8), WIDE:]
                    points.append((real, imag if f <= HALF else -imag))
                for n2, value in enumerate(swap(dft8(swap(points)))):
                    value = turn(value, -n2 * f1)
                    mid[n2 * 8 + f1, 0] = value[0]
                    mid[n2 * 8 + f1, 1] = value[1]
            for n2 in range(8):
                points = [(mid[n2 * 8 + f1, 0], mid[n2 * 8 + f1, 1]) for f1 in range(8)]
                for n1, value in enumerate(swap(dft8(swap(points)))):
                    n = 8 * n1 + n2
                    both = tile(c, q, n)
                    pout[n] += value[0] * both[:8] + value[1] * both[8:]
            pass

        if qs[-1] + 1 < PAIRS:
            return

        @pl.loop(0, BLOCKS // 2)
        def _(i):
            zk, row = i // 8 * 2 + i % 2, i // 2 % 4
            for w in range(2):
                whole = pout[2 * i + w]
                whole = whole + pltpu.roll(whole, 4, 0)
                if c < MIXED:
                    for s in range(XS):
                        rs_snd[c, s, zk, row, w : w + 1] = whole[s : s + 1]
                else:
                    whole = whole + pltpu.roll(whole, 2, 0)
                    whole = whole + pltpu.roll(whole, 1, 0)
                    qb[c - MIXED + 1][zk, 0, row, w : w + 1] = whole[:1]

    def send_sums(c):
        for d in range(1, XS):
            remote(rs_snd.at[c, xs[d]], rs_rcv.at[c, d - 1], rs_send.at[c], rs_recv.at[c], lon, mems[d])

    def parts(g):
        return ((0, 2), (2, 2)) if g == len(SETS) - 1 else ((0, 4),)

    def send_back(g):
        for j, c in enumerate(SETS[g]):
            if c < MIXED:
                done(rs_rcv.at[c], rs_recv.at[c])
                qb[g][:, j] = rs_snd[c, x] + rs_rcv[c, 0] + rs_rcv[c, 1] + rs_rcv[c, 2]
        mine, all_of = z * 2 + k, pl.ds(0, len(SETS[g]))
        for i, (row, count) in enumerate(parts(g)):
            rows, sem = pl.ds(row, count), ret_recv.at[g + i]
            for e in (1, 0):
                for s in range(8):
                    if e or s:
                        index = zs[s // 2] // 4 + ks[s % 2]
                        remote(
                            qb[g].at[index, all_of, rows], fr[g].at[zhi, mine, all_of, rows],
                            ret_send.at[g], sem, rows16[s], groups[e],
                        )
            local(qb[g].at[mine, all_of, rows], fr[g].at[zhi, mine, all_of, rows], sem)

    def send_all(g):
        for i, (first_row, count) in enumerate(parts(g)):
            rows = range(first_row, first_row + count)
            all_of = pl.ds(0, len(SETS[g]))
            arrived = fr[g].at[pl.ds(0, 2), pl.ds(0, 8), all_of, pl.ds(first_row, count)]
            done(arrived, ret_recv.at[g + i])
            for row in rows:
                for j in range(len(SETS[g])):
                    part[g][row, j] = fr[g][0, :, j, row] + fr[g][1, :, j, row]

            def send(row, d):
                there = z * 8 + row * 2 + k
                remote(part[g].at[row], fin[g].at[x, y], fin_send.at[g], fin_recv.at[g], there, mems[d])

            for d in (2, 1, 3):
                for row in rows:
                    send(row, d)
            for row in rows:
                pl.when(y != row)(functools.partial(send, row, 0))
        local(part[g].at[y], fin[g].at[x, y], fin_recv.at[g])

    def assemble(g):
        done(fin[g], fin_recv.at[g])

        @pl.loop(0, 4)
        def _(row):
            for j, c in enumerate(SETS[g]):
                for s in range(XS):
                    for i in range(8):
                        to, at = i // 2 * 8 + row * 2 + i % 2, c * PER + s
                        out[to, at : at + 1, :WIDE] = fin[g][s, row, j, i, 0:1]
                        out[to, at : at + 1, WIDE:] = fin[g][s, row, j, i, 1:2]

    for step in range(CHUNKS):
        if step < CHUNKS - 1:
            done(rcv.at[step], main_recv.at[step])
        if step < 2:
            send_main(step + 1, 1)
        if step < CHUNKS - 1:
            convolve(step, range(PAIRS))
        else:
            for q in range(PAIRS):
                done(rcv.at[step, pl.ds(0, LONS), pl.ds(q * 16, 16)], main_recv.at[step + q])
                convolve(step, (q,))
        if step < MIXED:
            send_sums(step)
        else:
            send_back(step - 1)
        if step < 2:
            rearrange_mixed(step + 2)
            send_main(step + 2, 0)
        if step == 2:
            send_main(3, 1)
            send_back(0)
            send_all(1)

    send_all(0)
    send_all(2)
    assemble(1)
    assemble(0)
    assemble(2)

    @pl.when(lon % XS == x)
    def _():
        done(inc_in.at[pl.ds(0, (LONS - 1) * LATS)], inc_send)

    done(incb.at[three], incx_send)
    for c in range(CHUNKS):
        done(snd.at[c, pl.ds(0, LONS - 1)], main_send.at[c])
        if c >= MIXED:
            done(xsnd.at[c - MIXED, three], x_send.at[c - MIXED])
        if c < MIXED:
            done(rs_rcv.at[c], rs_send.at[c])
    for g in range(len(SETS)):
        done(fr[g].at[0], ret_send.at[g])
        done(fr[g].at[0, pl.ds(0, 7)], ret_send.at[g])
        done(fin[g].at[three], fin_send.at[g])
        done(fin[g].at[0, three], fin_send.at[g])


def per_device(anomalies, increment, spectral_taper):
    hbm, vmem = pl.BlockSpec(memory_space=pltpu.HBM), pl.BlockSpec(memory_space=pltpu.VMEM)
    constants = tables()
    dma = pltpu.SemaphoreType.DMA
    circle = (8, 4, 2, WIDE)
    mixed = (max(CHUNKS - MIXED, 1), XS, LONS // 2, 2 * MEMBERS, 2 * WIDE)
    total = pl.pallas_call(
        kernel,
        out_shape=jax.ShapeDtypeStruct((LONS, LATS, 2 * WIDE), F32),
        in_specs=[hbm] * 7,
        out_specs=vmem,
        scratch_shapes=[
            pltpu.VMEM((MEMBERS, LONS * LATS, 2 * WIDE), BF16),
            pltpu.VMEM((LONS * LATS, 2 * WIDE), BF16),
            pltpu.VMEM((BLOCKS, WIDE), F32),
        ]
        + [pltpu.VMEM(t.shape, F32) for t in constants]
        + [
            pltpu.VMEM((CHUNKS, LONS, ROWS, 2 * WIDE), BF16),
            pltpu.VMEM((CHUNKS, LONS, ROWS, 2 * WIDE), BF16),
            pltpu.VMEM(mixed, BF16),
            pltpu.VMEM(mixed, BF16),
            pltpu.VMEM((XS, LONS // XS, LATS, 2 * WIDE), BF16),
            pltpu.VMEM((CHUNKS, BLOCKS, 8, WIDE), F32),
            pltpu.VMEM((2, 40, 2 * WIDE), F32),
            pltpu.VMEM((HALF + 1, WIDE, 2 * WIDE), BF16),
            pltpu.VMEM((BLOCKS, ROWS // 2, 2 * WIDE), F32),
            pltpu.VMEM((BLOCKS, 2, 8, WIDE), F32),
            pltpu.VMEM((BLOCKS, 8, WIDE), F32),
            pltpu.VMEM((CHUNKS, XS) + circle, F32),
            pltpu.VMEM((CHUNKS, XS - 1) + circle, F32),
            dma((8,)), dma, dma, dma, dma, dma((CHUNKS,)), dma((CHUNKS + 1,)),
            dma((CHUNKS,)), dma((CHUNKS,)), dma((CHUNKS,)), dma((CHUNKS,)), dma((CHUNKS,)), dma((CHUNKS,)),
            dma((CHUNKS,)), dma((CHUNKS,)), pltpu.SemaphoreType.REGULAR,
        ]
        + [pltpu.VMEM((8, len(g), 4, 2, WIDE), F32) for g in SETS]
        + [pltpu.VMEM((2, 8, len(g), 4, 2, WIDE), F32) for g in SETS]
        + [pltpu.VMEM((4, len(g), 8, 2, WIDE), F32) for g in SETS]
        + [pltpu.VMEM((XS, 4, len(g), 8, 2, WIDE), F32) for g in SETS],
        compiler_params=pltpu.CompilerParams(
            collective_id=0, has_side_effects=True, vmem_limit_bytes=62 << 20
        ),
        name="localize",
    )(anomalies, increment, spectral_taper.reshape(BLOCKS, WIDE), *constants)
    members = lax.axis_size("mem") * MEMBERS
    return total.reshape(LONS * LATS, 2 * WIDE) / (members - 1)


def solution(mesh):
    in_specs = (P("mem", None, "lon"), P(None, "lon"), P())
    return jax.shard_map(
        per_device, mesh=mesh, in_specs=in_specs, out_specs=P(None, "lon"), check_vma=False
    )
```

```python
import functools
import math

import jax
import jax.numpy as jnp
import numpy as np
from jax import lax
from jax.experimental import pallas as pl
from jax.experimental.pallas import tpu as pltpu
from jax.sharding import PartitionSpec as P

MESH = pl.DeviceIdType.MESH
NLON = 8192
BLOCKS = 64
WIDE = 128
HALF = BLOCKS // 2
LONS = 32
XS = 4
LATS = 16
CHUNKS = 4
SETS = ((0, 1), (2,), (3,))
MIXED = 2
PER = LATS // CHUNKS
MEMBERS = 8
ROWS = PER * MEMBERS
PAIRS = ROWS // 16
F32 = jnp.float32
BF16 = jnp.bfloat16


def tables():
    s = np.arange(WIDE)[:, None]
    r = np.arange(BLOCKS)[None, :]
    first = 2 * math.pi * (s * r % BLOCKS) / BLOCKS
    first = np.concatenate([np.cos(first), np.sin(first)], 0)
    c = np.arange(WIDE)[None, :]
    twist = 2 * math.pi * (s * c % NLON) / NLON
    twist = np.stack([np.cos(twist), np.sin(twist)])
    d = np.arange(BLOCKS)[:, None]
    back = 2 * math.pi * (d * c % BLOCKS) / BLOCKS
    back = np.stack([np.cos(back), np.sin(back)]) / (NLON * BLOCKS)
    f = np.arange(40)[:, None]
    d = np.arange(BLOCKS)[None, :]
    here = 2 * math.pi * (f * d % BLOCKS) / BLOCKS
    there = 2 * math.pi * (f * (d + 1) % BLOCKS) / BLOCKS
    again = np.stack([np.cos(here), -np.sin(here), np.cos(there), -np.sin(there)])
    return [np.asarray(t, np.float32) for t in (first, twist, back, again)]


def dft4(x):
    (ar, ai), (br, bi), (cr, ci), (dr, di) = x
    er, ei, fr, fi = ar + cr, ai + ci, ar - cr, ai - ci
    gr, gi, hr, hi = br + dr, bi + di, br - dr, bi - di
    return [(er + gr, ei + gi), (fr + hi, fi - hr), (er - gr, ei - gi), (fr - hi, fi + hr)]


def dft8(x):
    even, odd = dft4(x[0::2]), dft4(x[1::2])
    root = math.sqrt(0.5)
    (ar, ai), (br, bi), (cr, ci), (dr, di) = odd
    turned = [
        (ar, ai),
        ((br + bi) * root, (bi - br) * root),
        (ci, -cr),
        ((di - dr) * root, (dr + di) * -root),
    ]
    low = [(e[0] + t[0], e[1] + t[1]) for e, t in zip(even, turned)]
    high = [(e[0] - t[0], e[1] - t[1]) for e, t in zip(even, turned)]
    return low + high


def swap(x):
    return [(i, r) for r, i in x]


def turn(x, power):
    power = power % BLOCKS
    if power == 0:
        return x
    c = math.cos(2 * math.pi * power / BLOCKS)
    s = -math.sin(2 * math.pi * power / BLOCKS)
    return (x[0] * c - x[1] * s, x[0] * s + x[1] * c)


def high(a, b, dims=((1,), (0,))):
    return lax.dot_general(
        a, b, (dims, ((), ())), precision=lax.Precision.HIGHEST, preferred_element_type=F32
    )


def kernel(
    a_hbm, inc_hbm, taper_hbm, first_hbm, twist_hbm, back_hbm, again_hbm, out,
    a_in, inc_in, taper, first, twist, back, again,
    snd, rcv, xsnd, xrcv, incb, incf, lines, weights, spec, mid, pout, rs_snd, rs_rcv,
    load_sem, inc_send, inc_recv, incx_send, incx_recv, main_send, main_recv,
    x_send, x_recv, rs_send, rs_recv, ret_send, ret_recv, fin_send, fin_recv, group_sem, *sums,
):
    lon, mem = lax.axis_index("lon"), lax.axis_index("mem")
    z, y, k = lon // 8, (lon // 2) % 4, lon % 2
    zhi, x = mem // XS, mem % XS

    qb, fr, part, fin = [sums[i * len(SETS) : (i + 1) * len(SETS)] for i in range(4)]

    def load(source, target, sem):
        copy = pltpu.make_async_copy(source, target, load_sem.at[sem])
        copy.start()
        return copy

    group = MEMBERS // 2
    load_a = [load(a_hbm.at[pl.ds(j * group, group)], a_in.at[pl.ds(j * group, group)], j) for j in range(2)]

    def after(v, d):
        return (v + d) % 4

    zs = [after(z, d) * 8 for d in range(4)]
    ys = [after(y, d) * 2 for d in range(4)]
    ks = [k, 1 - k]
    peers = [zs[s // 8] + ys[s // 2 % 4] + ks[s % 2] for s in range(LONS)]
    xs = [(x + d) % XS for d in range(XS)]
    mems = [zhi * XS + xs[d] for d in range(XS)]
    groups = [mem, (1 - zhi) * XS + x]
    rows16 = [zs[s // 2] + ys[0] + ks[s % 2] for s in range(8)]

    barrier = pltpu.get_barrier_semaphore()

    def greet(there, group):
        pl.semaphore_signal(
            barrier, inc=1, device_id={"lon": there, "mem": group}, device_id_type=MESH
        )

    greet(lon, groups[1])
    for s in reversed(range(1, LONS)):
        greet(peers[s], mem)
    for d in range(1, XS):
        greet(lon, mems[d])

    load_i = load(inc_hbm, inc_in, 2)
    pairs = [(taper_hbm, taper), (first_hbm, first), (twist_hbm, twist), (back_hbm, back), (again_hbm, again)]
    load_t = [load(a, b, 3 + i) for i, (a, b) in enumerate(pairs)]

    def remote(source, target, send, recv, there, group):
        pltpu.make_async_remote_copy(
            src_ref=source, dst_ref=target, send_sem=send, recv_sem=recv,
            device_id={"lon": there, "mem": group}, device_id_type=MESH,
        ).start()

    def local(source, target, sem):
        pltpu.make_async_copy(source, target, sem).start()

    def done(ref, sem):
        pltpu.make_async_copy(ref, ref, sem).wait()

    wanted = lax.broadcasted_iota(jnp.int32, (8, WIDE), 0)
    upper = wanted < PER

    def rearrange(c):
        half, low = c // 2, c % 2 == 0

        @pl.loop(0, LONS)
        def _(t):
            for w in range(2):
                cols = slice(w * WIDE, (w + 1) * WIDE)
                parts = []
                for j in range(MEMBERS):
                    whole = a_in[j, pl.ds(t * LATS, LATS), cols].astype(F32)
                    parts.append(whole[half * 8 : half * 8 + 8])
                for j in range(0, MEMBERS, 4):
                    rows = []
                    for i in (j, j + 2):
                        one, two = parts[i], parts[i + 1]
                        if low:
                            two = pltpu.roll(two, PER, 0)
                        else:
                            one = pltpu.roll(one, PER, 0)
                        rows.append(jnp.where(upper, one, two))
                    snd[c, t, pl.ds(j * PER, 4 * PER), cols] = jnp.concatenate(rows).astype(BF16)

    def gather_x():
        row = lax.broadcasted_iota(jnp.int32, (XS * MEMBERS, MEMBERS * LATS), 0)
        col = lax.broadcasted_iota(jnp.int32, (XS * MEMBERS, MEMBERS * LATS), 1)
        for c in range(MIXED, CHUNKS):
            pick = (col == row % MEMBERS * LATS + c * PER + row // MEMBERS).astype(BF16)

            @pl.loop(0, LONS // 2)
            def _(u):
                picked = []
                for e in range(2):
                    whole = a_in[:, pl.ds((2 * u + e) * LATS, LATS), :]
                    whole = whole.reshape(MEMBERS * LATS, 2 * WIDE)
                    picked.append(jnp.dot(pick, whole, preferred_element_type=F32))
                for s in range(XS):
                    both = [p[s * MEMBERS : (s + 1) * MEMBERS] for p in picked]
                    xsnd[c - MIXED, s, u] = jnp.concatenate(both).astype(BF16)

    def send_x(c):
        m = c - MIXED
        for d in range(1, XS):
            remote(xsnd.at[m, xs[d]], xrcv.at[m, x], x_send.at[m], x_recv.at[m], lon, mems[d])
        local(xsnd.at[m, x], xrcv.at[m, x], x_recv.at[m])

    def rearrange_mixed(c):
        m = c - MIXED
        done(xrcv.at[m], x_recv.at[m])

        @pl.loop(0, LONS // 2)
        def _(u):
            for s in range(0, XS, 2):
                one, two = xrcv[m, s, u].astype(F32), xrcv[m, s + 1, u].astype(F32)
                for e in range(2):
                    both = [v[e * MEMBERS : (e + 1) * MEMBERS] for v in (one, two)]
                    snd[c, 2 * u + e, s * MEMBERS : (s + 2) * MEMBERS] = jnp.concatenate(both).astype(BF16)

    def send_main(c, half):
        if c == CHUNKS - 1:
            rows, sem = pl.ds(half * 16, 16), main_recv.at[c + half]
            for s in range(1, LONS):
                remote(snd.at[c, peers[s], rows], rcv.at[c, lon, rows], main_send.at[c], sem, peers[s], mem)
            local(snd.at[c, lon, rows], rcv.at[c, lon, rows], sem)
            return
        for s in range(1, LONS):
            if s % 2 == half:
                remote(snd.at[c, peers[s]], rcv.at[c, lon], main_send.at[c], main_recv.at[c], peers[s], mem)
        if half:
            local(snd.at[c, lon], rcv.at[c, lon], main_recv.at[c])

    for copy in load_a:
        copy.wait()
    rearrange(0)
    load_i.wait()
    pl.semaphore_wait(barrier, LONS + XS - 1)
    pl.semaphore_signal(
        group_sem, inc=1, device_id={"lon": lon, "mem": groups[1]}, device_id_type=MESH
    )

    send_main(0, 0)
    pl.semaphore_wait(group_sem, 1)

    @pl.when(lon % XS == x)
    def _():
        for s in range(1, LONS):
            block = inc_in.at[pl.ds(peers[s] * LATS, LATS)]
            beyond = (z // 2 + peers[s] // 16) % 2
            there = (zhi + beyond) % 2 * XS + x
            remote(block, incb.at[x, lon // XS], inc_send, inc_recv, peers[s], there)
        local(inc_in.at[pl.ds(lon * LATS, LATS)], incb.at[x, lon // XS], inc_recv)

    send_main(0, 1)
    for c in range(1, MIXED):
        rearrange(c)
    gather_x()
    done(incb.at[x], inc_recv)
    for d in range(1, XS):
        remote(incb.at[x], incb.at[x], incx_send, incx_recv, lon, mems[d])
    for c in range(MIXED, CHUNKS):
        send_x(c)
    send_main(1, 0)

    for copy in load_t:
        copy.wait()

    u = high(first[...], taper[...])
    ur, ui = u[:WIDE], u[WIDE:]
    vr = ur * twist[0] - ui * twist[1]
    vi = ur * twist[1] + ui * twist[0]
    line = high(back[0], vr, ((1,), (1,))) - high(back[1], vi, ((1,), (1,)))
    lines[0, :, :WIDE] = high(again[0], line)
    lines[1, :, :WIDE] = high(again[1], line)
    lines[0, :, WIDE:] = high(again[2], line)
    lines[1, :, WIDE:] = high(again[3], line)

    @pl.loop(0, HALF + 1)
    def _(f):
        def toeplitz(part):
            row = jnp.broadcast_to(lines[part, pl.ds(f, 1), :], (WIDE, 2 * WIDE))
            return pltpu.roll(row, 0, 1, stride=1, stride_axis=0)[:, :WIDE]

        real, imag = toeplitz(0), toeplitz(1)
        weights[f, :, :WIDE] = real.astype(BF16)
        weights[f, :, WIDE:] = imag.astype(BF16)

    three = pl.ds(0, XS - 1)
    done(incb.at[three], incx_recv)

    @pl.loop(0, LONS)
    def _(i):
        for w in range(2):
            whole = incb[i % XS, i // XS, :, w * WIDE : (w + 1) * WIDE].astype(F32)
            for c in range(CHUNKS):
                part = whole[c // 2 * 8 : c // 2 * 8 + 8]
                turned = pltpu.roll(part, PER, 0)
                one, two = (part, turned) if c % 2 == 0 else (turned, part)
                if c < MIXED:
                    incf[c, 2 * i + w] = jnp.where(upper, one, two)
                else:
                    mine = jnp.where(wanted == c % 2 * PER + x, part, 0.0)
                    mine = jnp.sum(mine, axis=0, keepdims=True)
                    incf[c, 2 * i + w] = jnp.broadcast_to(mine, (8, WIDE))

    def tile(c, q, n):
        return rcv[c, n // 2, pl.ds(q * 16, 16), (n % 2) * WIDE : (n % 2 + 1) * WIDE].astype(F32)

    def convolve(c, qs):
        top, count = qs[0] * 8, len(qs) * 8
        @pl.loop(qs[0], qs[-1] + 1)
        def _(q):
            for n2 in range(8):
                points = []
                for n1 in range(8):
                    n = 8 * n1 + n2
                    both = tile(c, q, n)
                    field = incf[c, n]
                    real = (both[:8] * field).astype(BF16).astype(F32)
                    imag = (both[8:] * field).astype(BF16).astype(F32)
                    points.append((real, imag))
                for f1, value in enumerate(dft8(points)):
                    value = turn(value, n2 * f1)
                    mid[f1 * 8 + n2, 0] = value[0]
                    mid[f1 * 8 + n2, 1] = value[1]
            for f1 in range(8):
                points = [(mid[f1 * 8 + n2, 0], mid[f1 * 8 + n2, 1]) for n2 in range(8)]
                for f2, value in enumerate(dft8(points)):
                    f = f1 + 8 * f2
                    spec[f, pl.ds(q * 8, 8), :WIDE] = value[0]
                    spec[f, pl.ds(q * 8, 8), WIDE:] = value[1] if f <= HALF else -value[1]
            pass

        for f in range(HALF + 1):
            both = [f] if f in (0, HALF) else [f, BLOCKS - f]
            rows = len(both) * count
            reals = [spec[g, top : top + count, :WIDE] for g in both]
            imags = [spec[g, top : top + count, WIDE:] for g in both]
            value = jnp.concatenate(reals + imags).astype(BF16)
            value = jnp.dot(value, weights[f], preferred_element_type=F32)
            real = value[:rows, :WIDE] - value[rows:, WIDE:]
            imag = value[:rows, WIDE:] + value[rows:, :WIDE]
            for i, g in enumerate(both):
                spec[g, top : top + count, :WIDE] = real[i * count : (i + 1) * count]
                spec[g, top : top + count, WIDE:] = imag[i * count : (i + 1) * count]

        if top == 0:
            pout[...] = jnp.zeros_like(pout)

        @pl.loop(qs[0], qs[-1] + 1)
        def _(q):
            for f1 in range(8):
                points = []
                for f2 in range(8):
                    f = f1 + 8 * f2
                    real = spec[f, pl.ds(q * 8, 8), :WIDE]
                    imag = spec[f, pl.ds(q * 8, 8), WIDE:]
                    points.append((real, imag if f <= HALF else -imag))
                for n2, value in enumerate(swap(dft8(swap(points)))):
                    value = turn(value, -n2 * f1)
                    mid[n2 * 8 + f1, 0] = value[0]
                    mid[n2 * 8 + f1, 1] = value[1]
            for n2 in range(8):
                points = [(mid[n2 * 8 + f1, 0], mid[n2 * 8 + f1, 1]) for f1 in range(8)]
                for n1, value in enumerate(swap(dft8(swap(points)))):
                    n = 8 * n1 + n2
                    both = tile(c, q, n)
                    pout[n] += value[0] * both[:8] + value[1] * both[8:]
            pass

        if qs[-1] + 1 < PAIRS:
            return

        @pl.loop(0, BLOCKS // 2)
        def _(i):
            zk, row = i // 8 * 2 + i % 2, i // 2 % 4
            for w in range(2):
                whole = pout[2 * i + w]
                whole = whole + pltpu.roll(whole, 4, 0)
                if c < MIXED:
                    for s in range(XS):
                        rs_snd[c, s, zk, row, w : w + 1] = whole[s : s + 1]
                else:
                    whole = whole + pltpu.roll(whole, 2, 0)
                    whole = whole + pltpu.roll(whole, 1, 0)
                    qb[c - MIXED + 1][zk, 0, row, w : w + 1] = whole[:1]

    def send_sums(c):
        for d in range(1, XS):
            remote(rs_snd.at[c, xs[d]], rs_rcv.at[c, d - 1], rs_send.at[c], rs_recv.at[c], lon, mems[d])

    def parts(g):
        return ((0, 3), (3, 1)) if g == len(SETS) - 1 else ((0, 4),)

    def send_back(g):
        for j, c in enumerate(SETS[g]):
            if c < MIXED:
                done(rs_rcv.at[c], rs_recv.at[c])
                qb[g][:, j] = rs_snd[c, x] + rs_rcv[c, 0] + rs_rcv[c, 1] + rs_rcv[c, 2]
        mine, all_of = z * 2 + k, pl.ds(0, len(SETS[g]))
        for i, (row, count) in enumerate(parts(g)):
            rows, sem = pl.ds(row, count), ret_recv.at[g + i]
            for e in (1, 0):
                for s in range(8):
                    if e or s:
                        index = zs[s // 2] // 4 + ks[s % 2]
                        remote(
                            qb[g].at[index, all_of, rows], fr[g].at[zhi, mine, all_of, rows],
                            ret_send.at[g], sem, rows16[s], groups[e],
                        )
            local(qb[g].at[mine, all_of, rows], fr[g].at[zhi, mine, all_of, rows], sem)

    def send_all(g):
        for i, (first_row, count) in enumerate(parts(g)):
            rows = range(first_row, first_row + count)
            all_of = pl.ds(0, len(SETS[g]))
            arrived = fr[g].at[pl.ds(0, 2), pl.ds(0, 8), all_of, pl.ds(first_row, count)]
            done(arrived, ret_recv.at[g + i])
            for row in rows:
                for j in range(len(SETS[g])):
                    part[g][row, j] = fr[g][0, :, j, row] + fr[g][1, :, j, row]

            def send(row, d):
                there = z * 8 + row * 2 + k
                remote(part[g].at[row], fin[g].at[x, y], fin_send.at[g], fin_recv.at[g], there, mems[d])

            for d in (2, 1, 3):
                for row in rows:
                    send(row, d)
            for row in rows:
                pl.when(y != row)(functools.partial(send, row, 0))
        local(part[g].at[y], fin[g].at[x, y], fin_recv.at[g])

    def assemble(g):
        done(fin[g], fin_recv.at[g])

        @pl.loop(0, 4)
        def _(row):
            for j, c in enumerate(SETS[g]):
                for s in range(XS):
                    for i in range(8):
                        to, at = i // 2 * 8 + row * 2 + i % 2, c * PER + s
                        out[to, at : at + 1, :WIDE] = fin[g][s, row, j, i, 0:1]
                        out[to, at : at + 1, WIDE:] = fin[g][s, row, j, i, 1:2]

    for step in range(CHUNKS):
        if step < CHUNKS - 1:
            done(rcv.at[step], main_recv.at[step])
        if step < 2:
            send_main(step + 1, 1)
        if step < CHUNKS - 1:
            convolve(step, range(PAIRS))
        else:
            for q in range(PAIRS):
                done(rcv.at[step, pl.ds(0, LONS), pl.ds(q * 16, 16)], main_recv.at[step + q])
                convolve(step, (q,))
        if step < MIXED:
            send_sums(step)
        else:
            send_back(step - 1)
        if step < 2:
            rearrange_mixed(step + 2)
            send_main(step + 2, 0)
        if step == 2:
            send_main(3, 1)
            send_back(0)
            send_all(1)

    send_all(0)
    send_all(2)
    assemble(1)
    assemble(0)
    assemble(2)

    @pl.when(lon % XS == x)
    def _():
        done(inc_in.at[pl.ds(0, (LONS - 1) * LATS)], inc_send)

    done(incb.at[three], incx_send)
    for c in range(CHUNKS):
        done(snd.at[c, pl.ds(0, LONS - 1)], main_send.at[c])
        if c >= MIXED:
            done(xsnd.at[c - MIXED, three], x_send.at[c - MIXED])
        if c < MIXED:
            done(rs_rcv.at[c], rs_send.at[c])
    for g in range(len(SETS)):
        done(fr[g].at[0], ret_send.at[g])
        done(fr[g].at[0, pl.ds(0, 7)], ret_send.at[g])
        done(fin[g].at[three], fin_send.at[g])
        done(fin[g].at[0, three], fin_send.at[g])


def per_device(anomalies, increment, spectral_taper):
    hbm, vmem = pl.BlockSpec(memory_space=pltpu.HBM), pl.BlockSpec(memory_space=pltpu.VMEM)
    constants = tables()
    dma = pltpu.SemaphoreType.DMA
    circle = (8, 4, 2, WIDE)
    mixed = (max(CHUNKS - MIXED, 1), XS, LONS // 2, 2 * MEMBERS, 2 * WIDE)
    total = pl.pallas_call(
        kernel,
        out_shape=jax.ShapeDtypeStruct((LONS, LATS, 2 * WIDE), F32),
        in_specs=[hbm] * 7,
        out_specs=vmem,
        scratch_shapes=[
            pltpu.VMEM((MEMBERS, LONS * LATS, 2 * WIDE), BF16),
            pltpu.VMEM((LONS * LATS, 2 * WIDE), BF16),
            pltpu.VMEM((BLOCKS, WIDE), F32),
        ]
        + [pltpu.VMEM(t.shape, F32) for t in constants]
        + [
            pltpu.VMEM((CHUNKS, LONS, ROWS, 2 * WIDE), BF16),
            pltpu.VMEM((CHUNKS, LONS, ROWS, 2 * WIDE), BF16),
            pltpu.VMEM(mixed, BF16),
            pltpu.VMEM(mixed, BF16),
            pltpu.VMEM((XS, LONS // XS, LATS, 2 * WIDE), BF16),
            pltpu.VMEM((CHUNKS, BLOCKS, 8, WIDE), F32),
            pltpu.VMEM((2, 40, 2 * WIDE), F32),
            pltpu.VMEM((HALF + 1, WIDE, 2 * WIDE), BF16),
            pltpu.VMEM((BLOCKS, ROWS // 2, 2 * WIDE), F32),
            pltpu.VMEM((BLOCKS, 2, 8, WIDE), F32),
            pltpu.VMEM((BLOCKS, 8, WIDE), F32),
            pltpu.VMEM((CHUNKS, XS) + circle, F32),
            pltpu.VMEM((CHUNKS, XS - 1) + circle, F32),
            dma((8,)), dma, dma, dma, dma, dma((CHUNKS,)), dma((CHUNKS + 1,)),
            dma((CHUNKS,)), dma((CHUNKS,)), dma((CHUNKS,)), dma((CHUNKS,)), dma((CHUNKS,)), dma((CHUNKS,)),
            dma((CHUNKS,)), dma((CHUNKS,)), pltpu.SemaphoreType.REGULAR,
        ]
        + [pltpu.VMEM((8, len(g), 4, 2, WIDE), F32) for g in SETS]
        + [pltpu.VMEM((2, 8, len(g), 4, 2, WIDE), F32) for g in SETS]
        + [pltpu.VMEM((4, len(g), 8, 2, WIDE), F32) for g in SETS]
        + [pltpu.VMEM((XS, 4, len(g), 8, 2, WIDE), F32) for g in SETS],
        compiler_params=pltpu.CompilerParams(
            collective_id=0, has_side_effects=True, vmem_limit_bytes=62 << 20
        ),
        name="localize",
    )(anomalies, increment, spectral_taper.reshape(BLOCKS, WIDE), *constants)
    members = lax.axis_size("mem") * MEMBERS
    return total.reshape(LONS * LATS, 2 * WIDE) / (members - 1)


def solution(mesh):
    in_specs = (P("mem", None, "lon"), P(None, "lon"), P())
    return jax.shard_map(
        per_device, mesh=mesh, in_specs=in_specs, out_specs=P(None, "lon"), check_vma=False
    )
```
